256 devices in a mesh: row: 16 (over z, core), col: 8 (over x_hi, y), samp: 2 (over x_lo).
Axes of the slice: x: 4 (x_hi: 2, x_lo: 2; x = x_hi * 2 + x_lo), y: 4, z: 8, core: 2. Of those that a mesh axis runs over, the one named last changes fastest.
Arguments:
- acts: bfloat16 [24, 1536, 768], P('samp', 'row'), may hold values from -9 to 9
- cond: bfloat16 [24, 1536, 384], P('samp', 'row'), may hold values from -6 to 6
- pair: bfloat16 [1536, 1536, 128], P(('row', 'samp'), 'col'), may hold values from -6 to 88
- chain_id: int32 [1536], replicated, may hold values from 0 to 7, never falling along the last dimension, each value on 1 to 384 neighbouring positions
- residue_mask: int32 [1536], replicated, may hold values 0 or 1
- w_bias: bfloat16 [128, 16], replicated, may hold values from -25 to 25
- chain_bias: float32 [16], P('col'), may hold values from -2 to 2
- ada1_scale: bfloat16 [384, 768], replicated, may hold values from -0.3125 to 0.3125
- ada1_shift: bfloat16 [384, 768], replicated, may hold values from -0.3125 to 0.3125
- w_qkvg: bfloat16 [4, 768, 768], P(None, None, 'col'), may hold values from -0.21875 to 0.21875
- w_out: bfloat16 [768, 768], replicated, may hold values from -0.21875 to 0.21875
- out_gate1: bfloat16 [384, 768], P(None, 'col'), may hold values from -0.3125 to 0.3125
- ada2_scale: bfloat16 [384, 768], replicated, may hold values from -0.3125 to 0.3125
- ada2_shift: bfloat16 [384, 768], replicated, may hold values from -0.3125 to 0.3125
- w_up: bfloat16 [2, 768, 1536], P(None, None, 'col'), may hold values from -0.21875 to 0.21875
- w_down: bfloat16 [1536, 768], P('col'), may hold values from -0.15625 to 0.15625
- out_gate2: bfloat16 [384, 768], P(None, 'col'), may hold values from -0.3125 to 0.3125
Outputs:
- block_out: bfloat16 [24, 1536, 768], P('samp', 'row', 'col')
The draws below stay inside these ranges and needn't reach their ends.
All inputs are finite; a program needn't handle non-finite values.
Results may differ from the reference program's by a relative error of at most 0.011.
Values may be sent and summed in bfloat16 or wider, within the bound.
No kernel may reach another device: no remote copies, remote signals or barrier semaphores. Data moves between devices by JAX's collectives and lax.ppermute only.
A program may use at most 128 MiB of HBM per device.

```python
import math
import jax
import jax.numpy as jnp
import numpy as np
from jax import lax

D = 768
HEADS = 16
DH = 48
CS = 384
CZ = 128
FFH = 1536
ROWS_DEV = 96
TOKENS = 1536
SAMPLES = 24


def draw_acts(key, part):
    key = jax.random.fold_in(key, 5)
    shape = (SAMPLES, TOKENS, D)
    ramp = jnp.arange(D).astype(jnp.float32) / (D - 1)
    base = jnp.clip(jax.random.normal(key, shape, jnp.float32), -6.0, 6.0)
    factor = 0.5 * jnp.power(3.0, ramp)
    return (base * factor[None, None, :]).astype(jnp.bfloat16)


def draw_pair(key, part):
    key = jax.random.fold_in(key, 11)
    shape = (TOKENS, TOKENS, CZ)
    return jnp.clip(jax.random.normal(key, shape, jnp.float32), -6.0, 6.0).astype(jnp.bfloat16)


def draw_w_bias(key, part):
    key = jax.random.fold_in(key, 23)
    return jnp.clip(0.4 * jax.random.normal(key, (CZ, HEADS), jnp.float32), -1.6, 1.6).astype(jnp.bfloat16)


def touch_ends(result, rng, least, largest):
    extent = result.shape
    place = [jax.random.randint(jax.random.fold_in(rng, axis), (), 0, extent[axis]) for axis in range(len(extent))]
    result = result.at[tuple(place)].set(least)
    longest = extent.index(max(extent))
    place[longest] = (place[longest] + 1) % extent[longest]
    return result.at[tuple(place)].set(largest)


def levels(key, dims, cuts, smallest, high):
    gain = 1.0
    for axis_at, blocks in cuts:
        draws = jax.random.uniform(jax.random.fold_in(jax.random.fold_in(key, 6), axis_at), (blocks,), jnp.float32, smallest / len(cuts), high / len(cuts))
        gain = gain * jnp.repeat(jnp.exp(draws), dims[axis_at] // blocks).reshape((-1,) + (1,) * (len(dims) - 1 - axis_at))
    return gain


def split_up(amount, total, limit, slope):
    loads = [(1 << 20) // math.isqrt(rank ** slope) + 1 for rank in range(2, amount + 1)]
    surplus, given = total - limit - (amount - 1), [1] * (amount - 1)
    while surplus > 0:
        free = [i for i in range(amount - 1) if given[i] < limit]
        whole, remaining = sum([loads[i] for i in free]), surplus
        for i in free:
            addition = min(limit - given[i], max(1, remaining * loads[i] // whole), surplus)
            given[i] = given[i] + addition
            surplus = surplus - addition
    return np.array([limit] + given)


def uneven(key, count, total, reach, slope):
    if count == 2:
        one = jax.random.randint(key, (), max(1, total - reach), min(reach, total - 1) + 1)
        return jnp.stack([one, total - one])
    tallies = jnp.asarray(split_up(count, total, reach, slope), jnp.int32)
    twos = (count - 1) // 2
    source_of, taker = tallies[1:1 + 2 * twos:2], tallies[2:2 + 2 * twos:2]
    room = jnp.minimum(source_of - 1, reach - taker)
    moved = jax.random.randint(jax.random.fold_in(key, 1), (twos,), 0, 1 << 20) % (room + 1)
    tallies = tallies.at[1:1 + 2 * twos:2].set(source_of - moved).at[2:2 + 2 * twos:2].set(taker + moved)
    return tallies[jax.random.permutation(jax.random.fold_in(key, 2), count)]


def gaussian(own_key, extent, spread, most, cuts=(), kind=jnp.bfloat16):
    factor_of = levels(own_key, extent, cuts, -0.22, 0.18) if cuts else 1.0
    values = jax.random.normal(own_key, extent, jnp.float32) * spread * factor_of
    return jnp.minimum(jnp.maximum(values, -most), most).astype(kind)


def setup_inputs(seed: int = 0) -> dict:
    streams_of = jax.random.split(jax.random.key(seed), 18)
    return {
        "acts": draw_acts(jax.random.fold_in(streams_of[17], 71), 0),
        "cond": gaussian(streams_of[1], (SAMPLES, TOKENS, CS), 1.0, 6.0, ((0, 2), (1, 16))),
        "pair": draw_pair(jax.random.fold_in(streams_of[17], 71), 0),
        "chain_id": jnp.searchsorted(jnp.cumsum(uneven(streams_of[3], 8, TOKENS, TOKENS // 4, 2)), jnp.arange(TOKENS), side="right").astype(jnp.int32),
        "residue_mask": touch_ends((jax.random.randint(streams_of[4], (TOKENS,), 0, 8) < 7).astype(jnp.int32), jax.random.fold_in(streams_of[4], 1), 0, 1),
        "w_bias": draw_w_bias(jax.random.fold_in(streams_of[17], 71), 0),
        "chain_bias": jnp.clip(jax.random.uniform(streams_of[6], (HEADS,), jnp.float32, -2.0, 2.0) * levels(streams_of[6], (HEADS,), ((0, 8),), -0.4, 0.0), -2.0, 2.0),
        "ada1_scale": gaussian(streams_of[7], (CS, D), CS ** -0.5, 0.3125),
        "ada1_shift": gaussian(streams_of[8], (CS, D), CS ** -0.5, 0.3125),
        "w_qkvg": gaussian(streams_of[9], (4, D, D), D ** -0.5, 0.21875, ((2, 8),)),
        "w_out": gaussian(streams_of[10], (D, D), D ** -0.5, 0.21875),
        "out_gate1": gaussian(streams_of[11], (CS, D), CS ** -0.5, 0.3125, ((1, 8),)),
        "ada2_scale": gaussian(streams_of[12], (CS, D), CS ** -0.5, 0.3125),
        "ada2_shift": gaussian(streams_of[13], (CS, D), CS ** -0.5, 0.3125),
        "w_up": gaussian(streams_of[14], (2, D, FFH), D ** -0.5, 0.21875, ((2, 8),)),
        "w_down": gaussian(streams_of[15], (FFH, D), FFH ** -0.5, 0.15625, ((0, 8),)),
        "out_gate2": gaussian(streams_of[16], (CS, D), CS ** -0.5, 0.3125, ((1, 8),)),
    }


epsilon = 1e-05

def normalize(values):
    row_mean = lax.optimization_barrier(jnp.mean(values, axis=-1, keepdims=True))
    row_square = lax.optimization_barrier(jnp.mean(values * values, axis=-1, keepdims=True))
    return (values - row_mean) * lax.rsqrt(row_square - row_mean * row_mean + epsilon)

def matmul(left, right):
    return jnp.dot(left, right, preferred_element_type=jnp.float32)

def reference(acts, cond, pair, chain_id, residue_mask, w_bias, chain_bias, ada1_scale, ada1_shift, w_qkvg, w_out, out_gate1, ada2_scale, ada2_shift, w_up, w_down, out_gate2):

    def bias_block(pair_rows):
        pair_norm = normalize(pair_rows.astype(jnp.float32)).astype(jnp.bfloat16)
        return jnp.einsum('ijc,ch->hij', pair_norm.astype(jnp.float32), w_bias.astype(jnp.float32)).astype(jnp.bfloat16)
    pair_blocks = pair.reshape(TOKENS // ROWS_DEV, ROWS_DEV, TOKENS, CZ)
    pair_bias = lax.map(bias_block, pair_blocks)
    pair_bias = jnp.transpose(pair_bias, (1, 0, 2, 3)).reshape(HEADS, TOKENS, TOKENS).astype(jnp.float32)
    positions = jnp.arange(TOKENS).astype(jnp.int32)
    same_chain = (chain_id[:, None] == chain_id[None, :]).astype(jnp.float32)
    active_keys = (residue_mask[None, :] == 1) | (positions[:, None] == positions[None, :])
    key_bias = pair_bias + chain_bias[:, None, None] * same_chain[None]
    scale_multiplier = 1.0 / math.sqrt(DH)

    def one_sample(input_rows):
        activation_rows, cond_rows = input_rows
        cond_norm = normalize(cond_rows.astype(jnp.float32)).astype(jnp.bfloat16)
        attn_input = (jax.nn.sigmoid(matmul(cond_norm, ada1_scale)) * normalize(activation_rows.astype(jnp.float32)) + matmul(cond_norm, ada1_shift)).astype(jnp.bfloat16)
        queries = matmul(attn_input, w_qkvg[0]).astype(jnp.bfloat16).reshape(TOKENS, HEADS, DH)
        keys = matmul(attn_input, w_qkvg[1]).astype(jnp.bfloat16).reshape(TOKENS, HEADS, DH)
        values = matmul(attn_input, w_qkvg[2]).astype(jnp.bfloat16).reshape(TOKENS, HEADS, DH)
        attn_gate = jax.nn.sigmoid(matmul(attn_input, w_qkvg[3]))
        logits = jnp.einsum('ihd,jhd->hij', queries.astype(jnp.float32), keys.astype(jnp.float32)) * scale_multiplier + key_bias
        logits = jnp.where(active_keys[None], logits, -1000000000.0)
        row_max = lax.optimization_barrier(jnp.max(logits, axis=-1, keepdims=True))
        exp_terms = jnp.exp(logits - row_max)
        weights = (exp_terms / lax.optimization_barrier(jnp.sum(exp_terms, axis=-1, keepdims=True))).astype(jnp.bfloat16)
        attended = jnp.einsum('hij,jhd->ihd', weights.astype(jnp.float32), values.astype(jnp.float32)).reshape(TOKENS, D)
        heads_out = (attn_gate * attended).astype(jnp.bfloat16)
        stream = activation_rows.astype(jnp.float32) + jax.nn.sigmoid(matmul(cond_norm, out_gate1)) * matmul(heads_out, w_out)
        ffn_input = (jax.nn.sigmoid(matmul(cond_norm, ada2_scale)) * normalize(stream) + matmul(cond_norm, ada2_shift)).astype(jnp.bfloat16)
        hidden = (jax.nn.silu(matmul(ffn_input, w_up[1])) * matmul(ffn_input, w_up[0])).astype(jnp.bfloat16)
        return (stream + jax.nn.sigmoid(matmul(cond_norm, out_gate2)) * matmul(hidden, w_down)).astype(jnp.bfloat16)
    return lax.map(one_sample, (acts, cond))
```

```python
import functools
import math

import jax
import jax.numpy as jnp
from jax import lax
from jax.experimental import pallas as pl
from jax.experimental.pallas import tpu as pltpu
from jax.sharding import Mesh, PartitionSpec as P

DH = 48
PIECE = 2 * DH
GROUP = 4
WIDE = GROUP * PIECE
EPS = 1e-05
LOG2E = math.log2(math.e)
MASKED = -1000000000.0
COL = ("xh", "y")
PLANE = ("xh", "y", "core")
VMEM = 56 * 1024 * 1024

FIRST = ((0, 128), (0, 256), (128, 256), (256, 384))
SECOND = ((0, 128), (128, 256), (128, 384), (256, 384))

f32 = jnp.float32
bf16 = jnp.bfloat16


def normalize(values):
    mean = jnp.mean(values, axis=-1, keepdims=True)
    square = jnp.mean(values * values, axis=-1, keepdims=True)
    return (values - mean) * lax.rsqrt(square - mean * mean + EPS)


def dot(left, right):
    return jnp.dot(left, right, preferred_element_type=f32)


def dot_t(left, right):
    return lax.dot_general(left, right, (((1,), (1,)), ((), ())), preferred_element_type=f32)


def params():
    return pltpu.CompilerParams(vmem_limit_bytes=VMEM)


def cost(micros):
    return pl.CostEstimate(flops=0, bytes_accessed=int(micros * 3_400_000), transcendentals=0)


def project_kernel(place, acts, cond, scale, shift, w, keep, send, wcat):
    first = place[0] == 0

    @pl.when(pl.program_id(0) == 0)
    def _():
        low = [w[n][:, :DH] for n in range(4)]
        high = [w[n][:, DH:] for n in range(4)]
        kept = [jnp.where(first, low[n], high[n]) for n in (1, 2, 0, 3)]
        sent = [jnp.where(first, high[n], low[n]) for n in (1, 2, 0, 3)]
        wcat[...] = jnp.concatenate(kept + sent, axis=1)

    rows = GROUP * acts.shape[1]
    x = acts[...].reshape(rows, acts.shape[2]).astype(f32)
    c = normalize(cond[...].reshape(rows, cond.shape[2]).astype(f32)).astype(bf16)
    a = (jax.nn.sigmoid(dot(c, scale[...])) * normalize(x) + dot(c, shift[...])).astype(bf16)
    y = dot(a, wcat[...])
    lane = lax.broadcasted_iota(jnp.int32, (1, WIDE), 1) % (2 * PIECE)
    is_query = (lane >= PIECE) & (lane < PIECE + DH)
    y = (y * jnp.where(is_query, LOG2E / math.sqrt(DH), 1.0)).astype(bf16)
    step = acts.shape[1]
    for n, out in enumerate((keep, send)):
        for part in range(2):
            at = (2 * n + part) * PIECE
            out[part] = jnp.concatenate(
                [y[j * step : (j + 1) * step, at : at + PIECE] for j in range(GROUP)], axis=1
            )


def project(core, acts, cond, scale, shift, w):
    samples, rows, width = acts.shape
    groups = samples // GROUP
    out = jax.ShapeDtypeStruct((2, rows, samples * PIECE), bf16)
    whole = lambda shape: pl.BlockSpec(shape, lambda g, p: (0,) * len(shape))
    return pl.pallas_call(
        project_kernel,
        grid_spec=pltpu.PrefetchScalarGridSpec(
            num_scalar_prefetch=1,
            grid=(groups,),
            in_specs=[
                pl.BlockSpec((GROUP, rows, width), lambda g, p: (g, 0, 0)),
                pl.BlockSpec((GROUP, rows, cond.shape[2]), lambda g, p: (g, 0, 0)),
                whole(scale.shape),
                whole(shift.shape),
                whole(w.shape),
            ],
            out_specs=[pl.BlockSpec((2, rows, WIDE), lambda g, p: (0, 0, g))] * 2,
            scratch_shapes=[pltpu.VMEM((width, WIDE), bf16)],
        ),
        out_shape=[out, out],
        compiler_params=params(),
        cost_estimate=cost(8),
        name="project",
    )(core, acts, cond, scale, shift, w)


def bias_kernel(pair, w, out, left, right):
    step = pl.program_id(0)
    heads = w.shape[0]
    rows = left.shape[0] // heads
    spare = jnp.zeros((heads, 256 - out.shape[1]), f32)
    for i in range(pair.shape[0]):
        x = normalize(pair[i].astype(f32)).astype(bf16)
        t = dot_t(w[...], x)
        at = pl.ds(step * pair.shape[0] + i, heads, stride=rows)
        left[at, :] = t[:, :128]
        right[at, :] = jnp.concatenate([t[:, 128:], spare], axis=1)

    @pl.when(step == pl.num_programs(0) - 1)
    def _():
        both = jnp.concatenate([left[...], right[...]], axis=1)
        out[...] = both[:, : out.shape[1]].astype(bf16)


def tile_bias(pair, w_bias):
    rows, keys, width = pair.shape
    heads = w_bias.shape[1]
    block = 8
    flat = pl.pallas_call(
        bias_kernel,
        grid=(rows // block,),
        in_specs=[
            pl.BlockSpec((block, keys, width), lambda g: (g, 0, 0)),
            pl.BlockSpec((heads, width), lambda g: (0, 0)),
        ],
        out_specs=pl.BlockSpec((heads * rows, keys), lambda g: (0, 0)),
        out_shape=jax.ShapeDtypeStruct((heads * rows, keys), bf16),
        scratch_shapes=[pltpu.VMEM((heads * rows, 128), f32)] * 2,
        compiler_params=params(),
        cost_estimate=cost(6),
        name="tile_bias",
    )(pair, w_bias.T)
    return flat.reshape(heads, rows, keys)


def assemble_kernel(place, tile_a, tile_b, chain_a, chain_b, chain_q, mask_a, mask_b, cb, out):
    n = pl.program_id(0)
    keys = tile_a.shape[3]
    total = 2 * keys
    low = place[10] == 0

    def rows_of(tile):
        parts = []
        for k in range(2):
            both = tile[0, k].astype(f32)
            mine, theirs = both[: keys // 4], both[keys // 4 :]
            parts += [jnp.where(low, mine, theirs), jnp.where(low, theirs, mine)]
        return jnp.concatenate(parts, axis=0)

    bias = jnp.concatenate([rows_of(tile_a), rows_of(tile_b)], axis=1)
    chain_k = jnp.concatenate([chain_a[0], chain_b[0]], axis=1)
    mask_k = jnp.concatenate([mask_a[0], mask_b[0]], axis=1)
    row = lax.broadcasted_iota(jnp.int32, (keys, keys), 0)
    col = lax.broadcasted_iota(jnp.int32, (keys, keys), 1)
    chain_rows = jnp.sum(
        jnp.where(row == col, chain_q[0].astype(f32), 0.0), axis=1, keepdims=True
    )
    lane = lax.broadcasted_iota(jnp.int32, (1, total), 1)
    position = jnp.where(lane < keys, place[n] * keys, place[4 + n] * keys - keys) + lane
    query = place[8] * keys + lax.broadcasted_iota(jnp.int32, (keys, 1), 0)
    strength = cb[place[9]]
    bias = bias + jnp.where(chain_rows == chain_k.astype(f32), strength, 0.0)
    active = (mask_k == 1) | (query == position)
    out[0] = jnp.where(active, bias * LOG2E, MASKED)


def assemble(place, tiles, chain_id, residue_mask, chain_bias):
    chunks, cores, rows, keys = tiles.shape
    tile = lambda f: pl.BlockSpec((1, cores, rows, keys), f)
    line = lambda f: pl.BlockSpec((1, 1, keys), f)
    at_a4, at_b4 = (lambda n, p: (p[n], 0, 0, 0)), (lambda n, p: (p[4 + n], 0, 0, 0))
    at_a3, at_b3 = (lambda n, p: (p[n], 0, 0)), (lambda n, p: (p[4 + n], 0, 0))
    at_q3 = lambda n, p: (p[8], 0, 0)
    chain = chain_id.reshape(chunks, 1, keys)
    mask = residue_mask.reshape(chunks, 1, keys)
    return pl.pallas_call(
        assemble_kernel,
        grid_spec=pltpu.PrefetchScalarGridSpec(
            num_scalar_prefetch=1,
            grid=(chunks // 2,),
            in_specs=[
                tile(at_a4),
                tile(at_b4),
                line(at_a3),
                line(at_b3),
                line(at_q3),
                line(at_a3),
                line(at_b3),
                pl.BlockSpec(memory_space=pltpu.SMEM),
            ],
            out_specs=pl.BlockSpec((1, keys, 2 * keys), lambda n, p: (n, 0, 0)),
        ),
        out_shape=jax.ShapeDtypeStruct((chunks // 2, keys, 2 * keys), f32),
        compiler_params=params(),
        cost_estimate=cost(4),
        name="assemble",
    )(place, tiles, tiles, chain, chain, chain, mask, mask, chain_bias)


def attend_kernel(start, last, halves, *refs):
    qg_ref, own_ref = refs[0], refs[1]
    key_refs, refs = refs[1 : 1 + halves], refs[1 + halves :]
    bias_ref, refs = refs[0], refs[1:]
    if not start:
        o_in, ml_in = refs[0], refs[1]
        refs = refs[2:]
    kv = jnp.concatenate([ref[...] for ref in key_refs], axis=0)
    qg = qg_ref[...]
    bias = bias_ref[0]
    rows = qg.shape[0]
    lane = lax.broadcasted_iota(jnp.int32, (1, WIDE), 1)
    ml_lane = lax.broadcasted_iota(jnp.int32, (1, 128), 1)
    o_tiles = [jnp.zeros((rows, 128), f32) for _ in range(3)]
    ml = jnp.zeros((rows, 128), f32)
    for j in range(GROUP):
        a, b = FIRST[j]
        here = lane[:, a:b]
        chosen = (here >= PIECE * j) & (here < PIECE * j + DH)
        q = jnp.where(chosen, qg[:, a:b], jnp.zeros((), bf16))
        s = dot_t(q, kv[:, a:b]) + bias
        top = jnp.max(s, axis=1, keepdims=True)
        if not start:
            top_old = ml_in[0][:, j : j + 1]
            top = jnp.maximum(top, top_old)
            alpha = jnp.exp2(top_old - top)
        p = jnp.exp2(s - top)
        total = jnp.sum(p, axis=1, keepdims=True)
        a, b = SECOND[j]
        o = dot(p.astype(bf16), kv[:, a:b])
        if not start:
            total = total + alpha * ml_in[0][:, GROUP + j : GROUP + j + 1]
            o = o + alpha * o_in[:, a:b]
        if last:
            out = refs[0]
            o = o / total * jax.nn.sigmoid(qg[:, a:b].astype(f32))
            shift = PIECE * j + DH - a
            if shift:
                o = pltpu.roll(o, (b - a) - shift, 1)
            o = o[:, :DH].astype(bf16)
            sample = pl.program_id(0) * GROUP + j
            part, inner = sample // 3, sample % 3
            size = rows // 4
            put = pl.ds(pl.multiple_of(inner * size, 16), size)
            for core in range(2):
                for half in range(2):
                    at = (core * 2 + half) * size
                    out[half * 8 + part * 2 + core, put, :] = o[at : at + size]
        else:
            for t in range(a // 128, b // 128):
                here = lane[:, 128 * t : 128 * t + 128]
                chosen = (here >= PIECE * j + DH) & (here < PIECE * j + PIECE)
                piece = o[:, 128 * t - a : 128 * t - a + 128]
                o_tiles[t] = jnp.where(chosen, piece, o_tiles[t])
            ml = jnp.where(ml_lane == j, top, ml)
            ml = jnp.where(ml_lane == GROUP + j, total, ml)
    if not last:
        o_out, ml_out = refs
        o_out[...] = jnp.concatenate(o_tiles, axis=1)
        ml_out[0] = ml


def attend(place, qg, parts, bias, pair, state, last):
    rows, width = qg.shape
    groups = width // WIDE
    start = state is None
    lanes = lambda n: pl.BlockSpec((n, WIDE), lambda g: (0, g))
    ml_spec = pl.BlockSpec((1, rows, 128), lambda g: (g, 0, 0))
    in_specs = [lanes(rows)] + [lanes(part.shape[0]) for part in parts]
    in_specs += [pl.BlockSpec((1,) + bias.shape[1:], lambda g: (pair, 0, 0))]
    args = [qg, *parts, bias]
    if not start:
        in_specs += [lanes(rows), ml_spec]
        args += list(state)
    if last:
        out_specs = pl.BlockSpec((16, 3 * rows // 4, DH), lambda g: (0, 0, 0))
        out_shape = jax.ShapeDtypeStruct((16, 3 * rows // 4, DH), bf16)
    else:
        out_specs = [lanes(rows), ml_spec]
        out_shape = [
            jax.ShapeDtypeStruct((rows, width), f32),
            jax.ShapeDtypeStruct((groups, rows, 128), f32),
        ]
    keys = sum(part.shape[0] for part in parts)
    return pl.pallas_call(
        functools.partial(attend_kernel, start, last, len(parts)),
        grid=(groups,),
        in_specs=in_specs,
        out_specs=out_specs,
        out_shape=out_shape,
        compiler_params=params(),
        cost_estimate=cost(7),
        name="attend_last" if last else "attend",
    )(*args)


def condition_kernel(place, cond, gates, scale, shift, out):
    rows = cond.shape[0] * cond.shape[1]
    width = cond.shape[2]
    c = normalize(cond[...].reshape(rows, width).astype(f32)).astype(bf16)
    gate = jnp.concatenate([gates[n % 4, n // 4] for n in range(8)], axis=0)
    out[0] = jax.nn.sigmoid(dot_t(c, gate[:, :width]))
    out[1] = jax.nn.sigmoid(dot(c, scale[...]))
    out[2] = dot(c, shift[...])
    out[3] = jax.nn.sigmoid(dot_t(c, gate[:, width:]))


def condition(place, cond, gathered, scale, shift):
    samples, rows, width = cond.shape
    model = scale.shape[1]
    take, size, share = samples // 4, rows // 2, model // 8
    at = gathered.shape[2] // share - 1
    return pl.pallas_call(
        condition_kernel,
        grid_spec=pltpu.PrefetchScalarGridSpec(
            num_scalar_prefetch=1,
            grid=(1,),
            in_specs=[
                pl.BlockSpec((take, size, width), lambda g, p: (p[2], p[1], 0)),
                pl.BlockSpec((4, 2, share, model), lambda g, p: (0, 0, at, 0)),
                pl.BlockSpec(scale.shape, lambda g, p: (0, 0)),
                pl.BlockSpec(shift.shape, lambda g, p: (0, 0)),
            ],
            out_specs=pl.BlockSpec((4, take * size, model), lambda g, p: (0, 0, 0)),
        ),
        out_shape=jax.ShapeDtypeStruct((4, take * size, model), f32),
        compiler_params=params(),
        cost_estimate=cost(4),
        name="condition",
    )(place, cond, gathered, scale, shift)


def transition_kernel(place, heads, acts, mix, w_out, mine, other, out, stream, inputs, acc):
    step = pl.program_id(0)
    first = place[0] == 0
    rows = stream.shape[0]

    @pl.when(step == 0)
    def _():
        x = jnp.concatenate(
            [heads[n] for n in range(heads.shape[0])], axis=1
        )
        s = acts[...].reshape(rows, acts.shape[2]).astype(f32) + mix[0] * dot(x, w_out[...])
        stream[...] = s
        inputs[...] = (mix[1] * normalize(s) + mix[2]).astype(bf16)
        acc[...] = jnp.zeros(acc.shape, f32)

    m, o = mine[0, 0], other[0, 0]
    half = m.shape[0] // 2
    low = half + half // 2
    x = inputs[...]
    a, b = dot_t(x, m[:half]), dot_t(x, o[:half])
    up, gate = jnp.where(first, a, b), jnp.where(first, b, a)
    hidden = (gate / (1.0 + jnp.exp(-gate)) * up).astype(bf16)
    md, od = m[half:low], o[half:low]
    down = jnp.concatenate([jnp.where(first, md, od), jnp.where(first, od, md)], axis=0)
    acc[...] += dot(hidden, down)

    @pl.when(step == pl.num_programs(0) - 1)
    def _():
        result = (stream[...] + mix[3] * acc[...]).astype(bf16)
        share = out.shape[2]
        for n in range(out.shape[0]):
            out[n] = result[:, n * share : (n + 1) * share]


def transition(place, heads, acts, mix, w_out, mine, other):
    samples, rows, width = acts.shape
    take, size = samples // 4, rows // 2
    block = pl.BlockSpec((1, 1) + mine.shape[2:], lambda g, p: (g // 2, g % 2, 0, 0))
    whole = lambda shape: pl.BlockSpec(shape, lambda g, p: (0,) * len(shape))
    return pl.pallas_call(
        transition_kernel,
        grid_spec=pltpu.PrefetchScalarGridSpec(
            num_scalar_prefetch=1,
            grid=(8,),
            in_specs=[
                whole(heads.shape),
                pl.BlockSpec((take, size, width), lambda g, p: (p[2], p[1], 0)),
                whole(mix.shape),
                whole(w_out.shape),
                block,
                block,
            ],
            out_specs=whole((8, take * size, width // 8)),
            scratch_shapes=[
                pltpu.VMEM((take * size, width), f32),
                pltpu.VMEM((take * size, width), bf16),
                pltpu.VMEM((take * size, width), f32),
            ],
        ),
        out_shape=jax.ShapeDtypeStruct((8, take * size, width // 8), bf16),
        compiler_params=params(),
        cost_estimate=cost(10),
        name="transition",
    )(place, heads, acts, mix, w_out, mine, other)


def per_device(
    acts,
    cond,
    pair,
    chain_id,
    residue_mask,
    w_bias,
    chain_bias,
    ada1_scale,
    ada1_shift,
    w_qkvg,
    w_out,
    out_gate1,
    ada2_scale,
    ada2_shift,
    w_up,
    w_down,
    out_gate2,
):
    z, core, xh, y, samp = (lax.axis_index(n) for n in ("z", "core", "xh", "y", "samp"))
    samples, rows, width = acts.shape
    swap = [(0, 1), (1, 0)]
    here = jnp.stack([core, xh, y]).astype(jnp.int32)

    def half_of(array, axis):
        size = array.shape[axis] // 2
        return lax.dynamic_slice_in_dim(array, core * size, size, axis)

    pack = jnp.concatenate(
        [
            lax.dynamic_index_in_dim(w_up, core, 0, keepdims=False).T,
            half_of(w_down, 0),
            jnp.concatenate([out_gate1.T, out_gate2.T], axis=1),
        ],
        axis=0,
    )
    far = lax.ppermute(pack, "xh", swap)

    tile = tile_bias(pair, w_bias)
    tile_other = lax.ppermute(tile, "samp", swap)

    keep, send = project(here, acts, cond, ada1_scale, ada1_shift, w_qkvg)
    send, tile_other = lax.optimization_barrier((send, tile_other))
    got = lax.ppermute(send, "core", swap)
    got, far = lax.optimization_barrier((got, far))
    lower = core == 0
    chip = jnp.concatenate(
        [jnp.where(lower, keep, got), jnp.where(lower, got, keep)], axis=1
    )
    chunk, qg = chip[0], chip[1]

    packs = jnp.where(xh == 0, jnp.stack([pack, far]), jnp.stack([far, pack]))
    mine = lax.all_gather(packs, "y", axis=0)

    tiles = jnp.concatenate([tile, tile_other], axis=1)
    tiles = lax.all_to_all(tiles, PLANE, split_axis=0, concat_axis=0, tiled=True)
    order = [(z + 8 - s) % 8 for s in (1, 2, 3, 8)] + [(z + s) % 8 for s in (1, 2, 3, 4)]
    place = jnp.stack(order + [z, core, samp]).astype(jnp.int32)
    tiles = tiles.reshape((8, 2) + tiles.shape[1:])
    bias = assemble(place, tiles, chain_id, residue_mask, chain_bias)

    up_ring = [(i, (i + 1) % 8) for i in range(8)]
    down_ring = [(i, (i + 7) % 8) for i in range(8)]
    half = chunk.shape[0] // 2
    right = left = chunk
    state = None
    for step in range(3):
        right = lax.ppermute(right, "z", up_ring)
        left = lax.ppermute(left, "z", down_ring)
        state = attend(place, qg, [right, left], bias, step, state, False)
    right = lax.ppermute(right[:half], "z", up_ring)
    left = lax.ppermute(left[half:], "z", down_ring)
    heads = attend(place, qg, [chunk, right, left], bias, 3, state, True)

    heads, mine = lax.optimization_barrier((heads, mine))
    other = lax.ppermute(mine, "core", swap)
    heads = lax.all_to_all(heads, PLANE, split_axis=0, concat_axis=0, tiled=True)
    mix = condition(here, cond, mine, ada2_scale, ada2_shift)
    out = transition(here, heads, acts, mix, w_out, mine, other)
    out = lax.all_to_all(out, COL, split_axis=0, concat_axis=0, tiled=True)
    out = out.reshape(2, 4, samples // 4, rows // 2, width // 8)
    return out.transpose(1, 2, 0, 3, 4).reshape(samples, rows, width // 8)


def solution(mesh):
    fine = Mesh(mesh.devices.reshape(8, 2, 2, 4, 2), ("z", "core", "xh", "y", "samp"))
    row = ("z", "core")
    in_specs = (
        P("samp", row, None),
        P("samp", row, None),
        P(row + ("samp",), COL, None),
        P(),
        P(),
        P(),
        P(COL),
        P(),
        P(),
        P(None, None, COL),
        P(),
        P(None, COL),
        P(),
        P(),
        P(None, None, COL),
        P(COL, None),
        P(None, COL),
    )
    return jax.shard_map(
        per_device,
        mesh=fine,
        in_specs=in_specs,
        out_specs=P("samp", row, COL),
        check_vma=False,
    )
```

```python
import functools
import math

import jax
import jax.numpy as jnp
from jax import lax
from jax.experimental import pallas as pl
from jax.experimental.pallas import tpu as pltpu
from jax.sharding import Mesh, PartitionSpec as P

DH = 48
PIECE = 2 * DH
GROUP = 4
WIDE = GROUP * PIECE
EPS = 1e-05
LOG2E = math.log2(math.e)
MASKED = -1000000000.0
COL = ("xh", "y")
PLANE = ("xh", "y", "core")
VMEM = 56 * 1024 * 1024

WINDOW = 256

f32 = jnp.float32
bf16 = jnp.bfloat16


def normalize(values):
    mean = jnp.mean(values, axis=-1, keepdims=True)
    square = jnp.mean(values * values, axis=-1, keepdims=True)
    return (values - mean) * lax.rsqrt(square - mean * mean + EPS)


def sigmoid(values):
    return 0.5 * jnp.tanh(0.5 * values) + 0.5


def dot(left, right):
    return jnp.dot(left, right, preferred_element_type=f32)


def dot_t(left, right):
    return lax.dot_general(left, right, (((1,), (1,)), ((), ())), preferred_element_type=f32)


def params():
    return pltpu.CompilerParams(vmem_limit_bytes=VMEM)


def cost(micros):
    return pl.CostEstimate(flops=0, bytes_accessed=int(micros * 3_400_000), transcendentals=0)


def project_kernel(place, acts, cond, scale, shift, w, keep, send, wcat):
    first = place[0] == 0

    @pl.when(pl.program_id(0) == 0)
    def _():
        low = [w[n, :DH] for n in range(4)]
        high = [w[n, DH:] for n in range(4)]
        kept = [jnp.where(first, low[n], high[n]) for n in (1, 2, 0, 3)]
        sent = [jnp.where(first, high[n], low[n]) for n in (1, 2, 0, 3)]
        wcat[...] = jnp.concatenate(kept + sent, axis=0)

    rows = GROUP * acts.shape[1]
    x = acts[...].reshape(rows, acts.shape[2]).astype(f32)
    c = normalize(cond[...].reshape(rows, cond.shape[2]).astype(f32)).astype(bf16)
    a = (sigmoid(dot(c, scale[...])) * normalize(x) + dot(c, shift[...])).astype(bf16)
    y = dot_t(a, wcat[...])
    lane = lax.broadcasted_iota(jnp.int32, (1, WIDE), 1) % (2 * PIECE)
    is_query = (lane >= PIECE) & (lane < PIECE + DH)
    y = (y * jnp.where(is_query, LOG2E / math.sqrt(DH), 1.0)).astype(bf16)
    step = acts.shape[1]
    for n, out in enumerate((keep, send)):
        for part in range(2):
            at = (2 * n + part) * PIECE
            out[part] = jnp.concatenate(
                [y[j * step : (j + 1) * step, at : at + PIECE] for j in range(GROUP)], axis=1
            )


def project(core, acts, cond, scale, shift, w):
    samples, rows, width = acts.shape
    groups = samples // GROUP
    out = jax.ShapeDtypeStruct((2, rows, samples * PIECE), bf16)
    whole = lambda shape: pl.BlockSpec(shape, lambda g, p: (0,) * len(shape))
    return pl.pallas_call(
        project_kernel,
        grid_spec=pltpu.PrefetchScalarGridSpec(
            num_scalar_prefetch=1,
            grid=(groups,),
            in_specs=[
                pl.BlockSpec((GROUP, rows, width), lambda g, p: (g, 0, 0)),
                pl.BlockSpec((GROUP, rows, cond.shape[2]), lambda g, p: (g, 0, 0)),
                whole(scale.shape),
                whole(shift.shape),
                whole(w.shape),
            ],
            out_specs=[pl.BlockSpec((2, rows, WIDE), lambda g, p: (0, 0, g))] * 2,
            scratch_shapes=[pltpu.VMEM((WIDE, width), bf16)],
        ),
        out_shape=[out, out],
        compiler_params=params(),
        cost_estimate=cost(8),
        name="project",
    )(core, acts, cond, scale, shift, w)


def bias_kernel(pair, w, out, left, right):
    step = pl.program_id(0)
    heads = w.shape[0]
    rows = left.shape[0] // heads
    spare = jnp.zeros((heads, 256 - out.shape[2]), f32)
    for i in range(pair.shape[0]):
        x = normalize(pair[i].astype(f32)).astype(bf16)
        t = dot_t(w[...], x)
        at = pl.ds(step * pair.shape[0] + i, heads, stride=rows)
        left[at, :] = t[:, :128]
        right[at, :] = jnp.concatenate([t[:, 128:], spare], axis=1)

    @pl.when(step == pl.num_programs(0) - 1)
    def _():
        both = jnp.concatenate([left[...], right[...]], axis=1)
        both = both[:, : out.shape[2]].astype(bf16)
        out[0] = both
        out[1] = both


def tile_bias(pair, w_bias):
    rows, keys, width = pair.shape
    heads = w_bias.shape[1]
    block = 8
    flat = pl.pallas_call(
        bias_kernel,
        grid=(rows // block,),
        in_specs=[
            pl.BlockSpec((block, keys, width), lambda g: (g, 0, 0)),
            pl.BlockSpec((heads, width), lambda g: (0, 0)),
        ],
        out_specs=pl.BlockSpec((2, heads * rows, keys), lambda g: (0, 0, 0)),
        out_shape=jax.ShapeDtypeStruct((2, heads * rows, keys), bf16),
        scratch_shapes=[pltpu.VMEM((heads * rows, 128), f32)] * 2,
        compiler_params=params(),
        cost_estimate=cost(6),
        name="tile_bias",
    )(pair, w_bias.T)
    return flat.reshape(2 * heads, rows, keys)


def assemble_kernel(place, *refs):
    tiles, chains, masks = refs[:2], refs[2:4], refs[4:6]
    chain_q, cb, out = refs[6:]
    keys = out.shape[1]
    row = lax.broadcasted_iota(jnp.int32, (keys, keys), 0)
    col = lax.broadcasted_iota(jnp.int32, (keys, keys), 1)

    def upright(line):
        return jnp.sum(jnp.where(row == col, line.astype(f32), 0.0), axis=1, keepdims=True)

    query = place[8] * keys + col
    for n in range(2):
        tile = tiles[n]
        parts = [tile[half, 0, core] for core in range(2) for half in range(2)]
        bias = jnp.concatenate(parts, axis=0).astype(f32).T
        same = upright(chains[n][0]) == chain_q[0].astype(f32)
        bias = bias + jnp.where(same, cb[place[9]], 0.0)
        key = place[2 * pl.program_id(0) + n] * keys + row
        active = (upright(masks[n][0]) == 1.0) | (query == key)
        bias = jnp.where(active, bias * LOG2E, MASKED)
        out[n] = jnp.concatenate([bias, bias], axis=1)


def assemble(place, tiles, chain_id, residue_mask, chain_bias):
    halves, chunks, cores, rows, keys = tiles.shape
    tile = [
        pl.BlockSpec((halves, 1, cores, rows, keys), lambda n, p, m=m: (0, p[2 * n + m], 0, 0, 0))
        for m in range(2)
    ]
    line = [pl.BlockSpec((1, 1, keys), lambda n, p, m=m: (p[2 * n + m], 0, 0)) for m in range(2)]
    own = pl.BlockSpec((1, 1, keys), lambda n, p: (p[8], 0, 0))
    chain = chain_id.reshape(chunks, 1, keys)
    mask = residue_mask.reshape(chunks, 1, keys)
    return pl.pallas_call(
        assemble_kernel,
        grid_spec=pltpu.PrefetchScalarGridSpec(
            num_scalar_prefetch=1,
            grid=(chunks // 2,),
            in_specs=tile + line + line + [own, pl.BlockSpec(memory_space=pltpu.SMEM)],
            out_specs=pl.BlockSpec((2, keys, 2 * keys), lambda n, p: (n, 0, 0)),
        ),
        out_shape=jax.ShapeDtypeStruct((chunks, keys, 2 * keys), f32),
        compiler_params=params(),
        cost_estimate=cost(5),
        name="assemble",
    )(place, tiles, tiles, chain, chain, mask, mask, chain, chain_bias)


def attend_kernel(start, last, halves, chunks, *refs):
    qg_ref, refs = refs[0], refs[1:]
    key_refs, refs = refs[:halves], refs[halves:]
    bias_refs, refs = refs[:chunks], refs[chunks:]
    if not start:
        state, refs = refs[0], refs[1:]
    out = refs[0]
    rows = qg_ref.shape[0]
    bias = jnp.concatenate([ref[0] for ref in bias_refs], axis=0)
    lane = lax.broadcasted_iota(jnp.int32, (1, WINDOW), 1)
    wide = lax.broadcasted_iota(jnp.int32, (1, 2 * rows), 1)
    row = lax.broadcasted_iota(jnp.int32, (2 * DH, 1), 0)
    none = jnp.zeros((), bf16)
    size = rows // 4
    pieces = {}
    for pair in range(2 * qg_ref.shape[1] // WIDE):
        a = pair // 2 * WIDE + 128 * (pair % 2)
        base = 2 * PIECE * pair - a
        group, at = pair // 2, pair % 2
        keys = jnp.concatenate([ref[:, a : a + WINDOW] for ref in key_refs], axis=0)
        queries = qg_ref[:, a : a + WINDOW]

        def both(offset):
            ends = [base + offset, base + offset + PIECE]
            return jnp.concatenate(
                [jnp.where((lane >= n) & (lane < n + DH), queries, none) for n in ends], axis=0
            )

        s = dot_t(keys, both(0)) + bias
        top = jnp.max(s, axis=0, keepdims=True)
        if not start:
            top_old = state[group, at, DH : DH + 1]
            top = jnp.maximum(top, top_old)
            alpha = jnp.exp2(top_old - top)
        p = jnp.exp2(s - top)
        total = jnp.sum(p, axis=0, keepdims=True)
        source = base + DH + jnp.where(row < DH, row, row + PIECE - DH)
        select = jnp.where(lane == source, 1.0, 0.0).astype(bf16)
        values = dot_t(select, keys).astype(bf16)
        o = dot(values, p.astype(bf16))
        o = jnp.where(wide < rows, o[:DH], o[DH:])
        if not start:
            total = total + alpha * state[group, at, DH + 1 : DH + 2]
            o = o + alpha * state[group, at, :DH]
        if last:
            fold = (lane == base + DH + row[:DH]) | (lane == base + DH + PIECE + row[:DH])
            gate = dot_t(jnp.where(fold, 1.0, 0.0).astype(bf16), both(DH))
            o = (o / total * sigmoid(gate)).astype(bf16)
            for j in range(2):
                for quarter in range(4):
                    begin = j * rows + quarter * size
                    pieces[2 * pair + j, quarter] = o[:, begin : begin + size]
        else:
            out[group, at, :DH] = o
            out[group, at, DH:] = jnp.concatenate(
                [top, total, jnp.zeros((6, 2 * rows), f32)], axis=0
            )
    if last:
        for part in range(4):
            for quarter in range(4):
                core, half = quarter // 2, quarter % 2
                out[half * 8 + part * 2 + core] = jnp.concatenate(
                    [pieces[3 * part + n, quarter] for n in range(3)], axis=1
                )


def attend(qg, parts, bias, at, state, last):
    rows, width = qg.shape
    groups = width // WIDE
    lanes = lambda n: pl.BlockSpec((n, width if last else WIDE), lambda g: (0, g))
    state_shape = (groups, 2, DH + 8, 2 * rows)
    state_spec = pl.BlockSpec((groups if last else 1,) + state_shape[1:], lambda g: (g, 0, 0, 0))
    chunks = sum(part.shape[0] for part in parts) // bias.shape[1]
    in_specs = [lanes(rows)] + [lanes(part.shape[0]) for part in parts]
    in_specs += [
        pl.BlockSpec((1,) + bias.shape[1:], lambda g, n=n: (at + n, 0, 0)) for n in range(chunks)
    ]
    args = [qg, *parts] + [bias] * chunks
    if state is not None:
        in_specs += [state_spec]
        args += [state]
    if last:
        out_shape = jax.ShapeDtypeStruct((16, DH, 3 * rows // 4), bf16)
        out_specs = pl.BlockSpec(out_shape.shape, lambda g: (0, 0, 0))
    else:
        out_specs = state_spec
        out_shape = jax.ShapeDtypeStruct(state_shape, f32)
    return pl.pallas_call(
        functools.partial(attend_kernel, state is None, last, len(parts), chunks),
        grid=(1 if last else groups,),
        in_specs=in_specs,
        out_specs=out_specs,
        out_shape=out_shape,
        compiler_params=params(),
        cost_estimate=cost(3 + chunks),
        name="attend_last" if last else "attend",
    )(*args)


def condition_kernel(place, cond, gates, scale, shift, out):
    rows = cond.shape[0] * cond.shape[1]
    width = cond.shape[2]
    c = normalize(cond[...].reshape(rows, width).astype(f32)).astype(bf16)
    gate = jnp.concatenate([gates[n % 4, n // 4] for n in range(8)], axis=0)
    out[0] = sigmoid(dot_t(c, gate[:, :width]))
    out[1] = sigmoid(dot(c, scale[...]))
    out[2] = dot(c, shift[...])
    out[3] = sigmoid(dot_t(c, gate[:, width:]))


def condition(place, cond, gathered, scale, shift):
    samples, rows, width = cond.shape
    model = scale.shape[1]
    take, size, share = samples // 4, rows // 2, model // 8
    at = gathered.shape[2] // share - 1
    return pl.pallas_call(
        condition_kernel,
        grid_spec=pltpu.PrefetchScalarGridSpec(
            num_scalar_prefetch=1,
            grid=(1,),
            in_specs=[
                pl.BlockSpec((take, size, width), lambda g, p: (p[2], p[1], 0)),
                pl.BlockSpec((4, 2, share, model), lambda g, p: (0, 0, at, 0)),
                pl.BlockSpec(scale.shape, lambda g, p: (0, 0)),
                pl.BlockSpec(shift.shape, lambda g, p: (0, 0)),
            ],
            out_specs=pl.BlockSpec((4, take * size, model), lambda g, p: (0, 0, 0)),
        ),
        out_shape=jax.ShapeDtypeStruct((4, take * size, model), f32),
        compiler_params=params(),
        cost_estimate=cost(4),
        name="condition",
    )(place, cond, gathered, scale, shift)


def transition_kernel(place, heads, acts, mix, w_out, mine, other, out, stream, inputs, acc):
    step = pl.program_id(0)
    first = place[0] == 0
    rows = stream.shape[0]

    @pl.when(step == 0)
    def _():
        x = heads[...].reshape(w_out.shape[0], rows)
        attended = lax.dot_general(
            x, w_out[...], (((0,), (0,)), ((), ())), preferred_element_type=f32
        )
        s = acts[...].reshape(rows, acts.shape[2]).astype(f32) + mix[0] * attended
        stream[...] = s
        inputs[...] = (mix[1] * normalize(s) + mix[2]).astype(bf16)
        acc[...] = jnp.zeros(acc.shape, f32)

    half = mine.shape[2] // 2
    low = half + half // 2
    x = inputs[...]
    for n in range(mine.shape[1]):
        m, o = mine[0, n], other[0, n]
        a, b = dot_t(x, m[:half]), dot_t(x, o[:half])
        up, gate = jnp.where(first, a, b), jnp.where(first, b, a)
        hidden = (gate * sigmoid(gate) * up).astype(bf16)
        md, od = m[half:low], o[half:low]
        down = jnp.concatenate([jnp.where(first, md, od), jnp.where(first, od, md)], axis=0)
        acc[...] += dot(hidden, down)

    @pl.when(step == pl.num_programs(0) - 1)
    def _():
        result = (stream[...] + mix[3] * acc[...]).astype(bf16)
        share = out.shape[2]
        for n in range(out.shape[0]):
            out[n] = result[:, n * share : (n + 1) * share]


def transition(place, heads, acts, mix, w_out, mine, other):
    samples, rows, width = acts.shape
    take, size = samples // 4, rows // 2
    block = pl.BlockSpec((1,) + mine.shape[1:], lambda g, p: (g, 0, 0, 0))
    whole = lambda shape: pl.BlockSpec(shape, lambda g, p: (0,) * len(shape))
    return pl.pallas_call(
        transition_kernel,
        grid_spec=pltpu.PrefetchScalarGridSpec(
            num_scalar_prefetch=1,
            grid=(mine.shape[0],),
            in_specs=[
                whole(heads.shape),
                pl.BlockSpec((take, size, width), lambda g, p: (p[2], p[1], 0)),
                whole(mix.shape),
                whole(w_out.shape),
                block,
                block,
            ],
            out_specs=whole((8, take * size, width // 8)),
            scratch_shapes=[
                pltpu.VMEM((take * size, width), f32),
                pltpu.VMEM((take * size, width), bf16),
                pltpu.VMEM((take * size, width), f32),
            ],
        ),
        out_shape=jax.ShapeDtypeStruct((8, take * size, width // 8), bf16),
        compiler_params=params(),
        cost_estimate=cost(9),
        name="transition",
    )(place, heads, acts, mix, w_out, mine, other)


def per_device(
    acts,
    cond,
    pair,
    chain_id,
    residue_mask,
    w_bias,
    chain_bias,
    ada1_scale,
    ada1_shift,
    w_qkvg,
    w_out,
    out_gate1,
    ada2_scale,
    ada2_shift,
    w_up,
    w_down,
    out_gate2,
):
    z, core, xh, y, samp = (lax.axis_index(n) for n in ("z", "core", "xh", "y", "samp"))
    samples, rows, width = acts.shape
    swap = [(0, 1), (1, 0)]
    here = jnp.stack([core, xh, y]).astype(jnp.int32)

    half_down = w_down.shape[0] // 2
    pack = jnp.concatenate(
        [
            lax.dynamic_index_in_dim(w_up, core, 0, keepdims=False).T,
            lax.dynamic_slice_in_dim(w_down, core * half_down, half_down, 0),
            jnp.concatenate([out_gate1.T, out_gate2.T], axis=1),
        ],
        axis=0,
    )
    far = lax.ppermute(pack, "xh", swap)
    tile = tile_bias(pair, w_bias)
    keep, send = project(here, acts, cond, ada1_scale, ada1_shift, w_qkvg.swapaxes(1, 2))
    send, tile = lax.optimization_barrier((send, tile))
    got = lax.ppermute(send, "core", swap)
    got, far = lax.optimization_barrier((got, far))
    lower = core == 0
    chip = jnp.concatenate(
        [jnp.where(lower, keep, got), jnp.where(lower, got, keep)], axis=1
    )
    chunk, qg = chip[0], chip[1]

    packs = jnp.where(xh == 0, jnp.stack([pack, far]), jnp.stack([far, pack]))
    mine = lax.all_gather(packs, "y", axis=0)

    up_ring = [(i, (i + 1) % 8) for i in range(8)]
    down_ring = [(i, (i + 7) % 8) for i in range(8)]

    def around(right, left):
        return lax.ppermute(right, "z", up_ring), lax.ppermute(left, "z", down_ring)

    half = chunk.shape[0] // 2
    one = around(chunk, chunk)
    tiles = lax.all_to_all(tile, ("samp",) + PLANE, split_axis=0, concat_axis=0, tiled=True)
    tiles = tiles.reshape((2, 8, 2) + tiles.shape[1:])
    two = around(*one)
    (two, tiles) = lax.optimization_barrier((two, tiles))
    order = [z + 7, z + 1, z + 6, z + 2, z + 5, z + 3, z, z + 4]
    place = jnp.stack([n % 8 for n in order] + [z, core]).astype(jnp.int32)
    bias = assemble(place, tiles, chain_id, residue_mask, chain_bias)
    three = around(*two)
    state = attend(qg, [*one, *two], bias, 0, None, False)
    state, three = lax.optimization_barrier((state, three))
    four = around(three[0][:half], three[1][half:])
    state = attend(qg, [*three, chunk], bias, 4, state, False)
    heads = attend(qg, [*four], bias, 7, state, True)

    heads, mine = lax.optimization_barrier((heads, mine))
    other = lax.ppermute(mine, "core", swap)
    heads = lax.all_to_all(heads, PLANE, split_axis=0, concat_axis=0, tiled=True)
    mix = condition(here, cond, mine, ada2_scale, ada2_shift)
    out = transition(here, heads, acts, mix, w_out, mine, other)
    out = lax.all_to_all(out, COL, split_axis=0, concat_axis=0, tiled=True)
    out = out.reshape(2, 4, samples // 4, rows // 2, width // 8)
    return out.transpose(1, 2, 0, 3, 4).reshape(samples, rows, width // 8)


def solution(mesh):
    fine = Mesh(mesh.devices.reshape(8, 2, 2, 4, 2), ("z", "core", "xh", "y", "samp"))
    row = ("z", "core")
    in_specs = (
        P("samp", row, None),
        P("samp", row, None),
        P(row + ("samp",), COL, None),
        P(),
        P(),
        P(),
        P(COL),
        P(),
        P(),
        P(None, None, COL),
        P(),
        P(None, COL),
        P(),
        P(),
        P(None, None, COL),
        P(COL, None),
        P(None, COL),
    )
    return jax.shard_map(
        per_device,
        mesh=fine,
        in_specs=in_specs,
        out_specs=P("samp", row, COL),
        check_vma=False,
    )
```

```python
import functools
import math

import jax
import jax.numpy as jnp
from jax import lax
from jax.experimental import pallas as pl
from jax.experimental.pallas import tpu as pltpu
from jax.sharding import Mesh, PartitionSpec as P

DH = 48
PIECE = 2 * DH
GROUP = 4
WIDE = GROUP * PIECE
EPS = 1e-05
LOG2E = math.log2(math.e)
MASKED = -1000000000.0
COL = ("xh", "y")
PLANE = ("xh", "y", "core")
VMEM = 14 * 1024 * 1024

WINDOW = 256

f32 = jnp.float32
bf16 = jnp.bfloat16


def normalize(values):
    mean = jnp.mean(values, axis=-1, keepdims=True)
    square = jnp.mean(values * values, axis=-1, keepdims=True)
    return (values - mean) * lax.rsqrt(square - mean * mean + EPS)


def sigmoid(values):
    return 0.5 * jnp.tanh(0.5 * values) + 0.5


def dot(left, right):
    return jnp.dot(left, right, preferred_element_type=f32)


def dot_t(left, right):
    return lax.dot_general(left, right, (((1,), (1,)), ((), ())), preferred_element_type=f32)


def params(limit=VMEM):
    return pltpu.CompilerParams(vmem_limit_bytes=limit)


def cost(micros):
    return pl.CostEstimate(flops=0, bytes_accessed=int(micros * 3_400_000), transcendentals=0)


def project_kernel(place, acts, cond, scale, shift, w, stay, send, wcat):
    first = place[0] == 0

    @pl.when(pl.program_id(0) == 0)
    def _():
        low = [w[n, :DH] for n in range(4)]
        high = [w[n, DH:] for n in range(4)]
        kept = [jnp.where(first, low[n], high[n]) for n in (1, 2, 0, 3)]
        sent = [jnp.where(first, high[n], low[n]) for n in (1, 2, 0, 3)]
        wcat[...] = jnp.concatenate(kept + sent, axis=0)

    rows = GROUP * acts.shape[1]
    x = acts[...].reshape(rows, acts.shape[2]).astype(f32)
    c = normalize(cond[...].reshape(rows, cond.shape[2]).astype(f32)).astype(bf16)
    a = (sigmoid(dot(c, scale[...])) * normalize(x) + dot(c, shift[...])).astype(bf16)
    y = dot_t(a, wcat[...])
    lane = lax.broadcasted_iota(jnp.int32, (1, WIDE), 1) % (2 * PIECE)
    is_query = (lane >= PIECE) & (lane < PIECE + DH)
    y = (y * jnp.where(is_query, LOG2E / math.sqrt(DH), 1.0)).astype(bf16)
    step = acts.shape[1]
    for n, out in enumerate((send.at[0], stay, send.at[1], send.at[2])):
        at = n * PIECE
        out[...] = jnp.concatenate(
            [y[j * step : (j + 1) * step, at : at + PIECE] for j in range(GROUP)], axis=1
        )


def project(core, acts, cond, scale, shift, w):
    samples, rows, width = acts.shape
    groups = samples // GROUP
    one = jax.ShapeDtypeStruct((rows, samples * PIECE), bf16)
    three = jax.ShapeDtypeStruct((3,) + one.shape, bf16)
    whole = lambda shape: pl.BlockSpec(shape, lambda g, p: (0,) * len(shape))
    return pl.pallas_call(
        project_kernel,
        grid_spec=pltpu.PrefetchScalarGridSpec(
            num_scalar_prefetch=1,
            grid=(groups,),
            in_specs=[
                pl.BlockSpec((GROUP, rows, width), lambda g, p: (g, 0, 0)),
                pl.BlockSpec((GROUP, rows, cond.shape[2]), lambda g, p: (g, 0, 0)),
                whole(scale.shape),
                whole(shift.shape),
                whole(w.shape),
            ],
            out_specs=[
                pl.BlockSpec((rows, WIDE), lambda g, p: (0, g)),
                pl.BlockSpec((3, rows, WIDE), lambda g, p: (0, 0, g)),
            ],
            scratch_shapes=[pltpu.VMEM((WIDE, width), bf16)],
        ),
        out_shape=[one, three],
        compiler_params=params(56 * 1024 * 1024),
        cost_estimate=cost(8),
        name="project",
    )(core, acts, cond, scale, shift, w)


def bias_kernel(pair, w, out, left, right):
    step = pl.program_id(0)
    heads = w.shape[0]
    rows, keys = left.shape[0] // heads, pair.shape[1]
    spare = jnp.zeros((heads, 256 - keys), f32)
    for i in range(pair.shape[0]):
        x = normalize(pair[i].astype(f32)).astype(bf16)
        t = dot_t(w[...], x)
        at = pl.ds(step * pair.shape[0] + i, heads, stride=rows)
        left[at, :] = t[:, :128]
        right[at, :] = jnp.concatenate([t[:, 128:], spare], axis=1)

    @pl.when(step == pl.num_programs(0) - 1)
    def _():
        for h in range(heads):
            rest = right[h * rows : (h + 1) * rows]
            rest = jnp.concatenate([rest[: rows // 2, :64], rest[rows // 2 :, :64]], axis=1)
            tile = jnp.concatenate([left[h * rows : (h + 1) * rows], rest], axis=0).astype(bf16)
            out[h] = tile


def tile_bias(pair, w_bias):
    rows, keys, width = pair.shape
    heads = w_bias.shape[1]
    block = 8
    shape = (heads, rows * keys // 128, 128)
    return pl.pallas_call(
        bias_kernel,
        grid=(rows // block,),
        in_specs=[
            pl.BlockSpec((block, keys, width), lambda g: (g, 0, 0)),
            pl.BlockSpec((heads, width), lambda g: (0, 0)),
        ],
        out_specs=pl.BlockSpec(shape, lambda g: (0, 0, 0)),
        out_shape=jax.ShapeDtypeStruct(shape, bf16),
        scratch_shapes=[pltpu.VMEM((heads * rows, 128), f32)] * 2,
        compiler_params=params(),
        cost_estimate=cost(6),
        name="tile_bias",
    )(pair, w_bias.T)


def assemble_kernel(place, *refs):
    tiles, chains, masks = refs[:2], refs[2:4], refs[4:6]
    chain_q, cb, out = refs[6:]
    keys = out.shape[1]
    row = lax.broadcasted_iota(jnp.int32, (keys, keys), 0)
    col = lax.broadcasted_iota(jnp.int32, (keys, keys), 1)

    def upright(line):
        return jnp.sum(jnp.where(row == col, line.astype(f32), 0.0), axis=1, keepdims=True)

    query = place[8] * keys + col
    low = place[10] == 0
    for n in range(2):
        tile = tiles[n]
        parts = []
        for core in range(2):
            own, theirs = tile[0, core, 0].astype(f32), tile[0, core, 1].astype(f32)
            parts += [jnp.where(low, own, theirs), jnp.where(low, theirs, own)]
        rows = keys // 4
        first = jnp.concatenate([part[:rows] for part in parts], axis=0)
        rest = []
        for part in parts:
            rest += [part[rows:, :64], part[rows:, 64:]]
        bias = jnp.concatenate([first, jnp.concatenate(rest, axis=0)], axis=1).T
        same = upright(chains[n][0]) == chain_q[0].astype(f32)
        bias = bias + jnp.where(same, cb[place[9]], 0.0)
        key = place[2 * pl.program_id(0) + n] * keys + row
        active = (upright(masks[n][0]) == 1.0) | (query == key)
        bias = jnp.where(active, bias * LOG2E, MASKED)
        out[n] = jnp.concatenate([bias, bias], axis=1)


def assemble(place, tiles, chain_id, residue_mask, chain_bias):
    chunks, cores, halves, rows, lanes = tiles.shape
    keys = chain_id.shape[0] // chunks
    tile = [
        pl.BlockSpec((1, cores, halves, rows, lanes), lambda n, p, m=m: (p[2 * n + m], 0, 0, 0, 0))
        for m in range(2)
    ]
    line = [pl.BlockSpec((1, 1, keys), lambda n, p, m=m: (p[2 * n + m], 0, 0)) for m in range(2)]
    own = pl.BlockSpec((1, 1, keys), lambda n, p: (p[8], 0, 0))
    chain = chain_id.reshape(chunks, 1, keys)
    mask = residue_mask.reshape(chunks, 1, keys)
    return pl.pallas_call(
        assemble_kernel,
        grid_spec=pltpu.PrefetchScalarGridSpec(
            num_scalar_prefetch=1,
            grid=(chunks // 2,),
            in_specs=tile + line + line + [own, pl.BlockSpec(memory_space=pltpu.SMEM)],
            out_specs=pl.BlockSpec((2, keys, 2 * keys), lambda n, p: (n, 0, 0)),
        ),
        out_shape=jax.ShapeDtypeStruct((chunks, keys, 2 * keys), f32),
        compiler_params=params(),
        cost_estimate=cost(5),
        name="assemble",
    )(place, tiles, tiles, chain, chain, mask, mask, chain, chain_bias)


def attend_kernel(start, last, picks, begin, chunks, *refs):
    qg_ref, refs = refs[0], refs[1:]
    key_refs, refs = refs[: len(picks)], refs[len(picks) :]
    key_refs = [ref if n is None else ref.at[n] for ref, n in zip(key_refs, picks)]
    bias_ref, refs = refs[0], refs[1:]
    if not start:
        state, refs = refs[0], refs[1:]
    out = refs[0]
    rows = qg_ref.shape[0]
    bias = bias_ref[begin : begin + chunks].reshape(chunks * bias_ref.shape[1], 2 * rows)
    lane = lax.broadcasted_iota(jnp.int32, (1, WINDOW), 1)
    wide = lax.broadcasted_iota(jnp.int32, (1, 2 * rows), 1)
    row = lax.broadcasted_iota(jnp.int32, (2 * DH, 1), 0)
    none = jnp.zeros((), bf16)
    size = rows // 4
    pieces = {}
    for pair in range(2 * qg_ref.shape[1] // WIDE):
        a = pair // 2 * WIDE + 128 * (pair % 2)
        base = 2 * PIECE * pair - a
        group, at = pair // 2, pair % 2
        keys = jnp.concatenate([ref[:, a : a + WINDOW] for ref in key_refs], axis=0)
        queries = qg_ref[:, a : a + WINDOW]

        def both(offset):
            ends = [base + offset, base + offset + PIECE]
            return jnp.concatenate(
                [jnp.where((lane >= n) & (lane < n + DH), queries, none) for n in ends], axis=0
            )

        s = dot_t(keys, both(0)) + bias
        top = jnp.max(s, axis=0, keepdims=True)
        if not start:
            top_old = state[group, at, DH : DH + 1]
            top = jnp.maximum(top, top_old)
            alpha = jnp.exp2(top_old - top)
        p = jnp.exp2(s - top)
        total = jnp.sum(p, axis=0, keepdims=True)
        source = base + DH + jnp.where(row < DH, row, row + PIECE - DH)
        select = jnp.where(lane == source, 1.0, 0.0).astype(bf16)
        values = dot_t(select, keys).astype(bf16)
        o = dot(values, p.astype(bf16))
        o = jnp.where(wide < rows, o[:DH], o[DH:])
        if not start:
            total = total + alpha * state[group, at, DH + 1 : DH + 2]
            o = o + alpha * state[group, at, :DH]
        if last:
            fold = (lane == base + DH + row[:DH]) | (lane == base + DH + PIECE + row[:DH])
            gate = dot_t(jnp.where(fold, 1.0, 0.0).astype(bf16), both(DH))
            o = (o / total * sigmoid(gate)).astype(bf16)
            for j in range(2):
                for quarter in range(4):
                    first = j * rows + quarter * size
                    pieces[2 * pair + j, quarter] = o[:, first : first + size]
        else:
            out[group, at, :DH] = o
            out[group, at, DH:] = jnp.concatenate(
                [top, total, jnp.zeros((6, 2 * rows), f32)], axis=0
            )
    if last:
        for part in range(4):
            for quarter in range(4):
                core, half = quarter // 2, quarter % 2
                out[half * 8 + part * 2 + core] = jnp.concatenate(
                    [pieces[3 * part + n, quarter] for n in range(3)], axis=1
                )


def attend(qg, parts, bias, begin, state, last):
    rows, width = qg.shape
    parts, picks = zip(*parts)
    chunks = len(parts)
    args = [qg, *parts, bias] + ([] if state is None else [state])
    if last:
        out_shape = jax.ShapeDtypeStruct((16, DH, 3 * rows // 4), bf16)
    else:
        out_shape = jax.ShapeDtypeStruct((width // WIDE, 2, DH + 8, 2 * rows), f32)
    return pl.pallas_call(
        functools.partial(attend_kernel, state is None, last, picks, begin, chunks),
        in_specs=[pl.BlockSpec(memory_space=pltpu.VMEM)] * len(args),
        out_specs=pl.BlockSpec(memory_space=pltpu.VMEM),
        out_shape=out_shape,
        compiler_params=params(),
        cost_estimate=cost(2 + chunks),
        name="attend_last" if last else "attend",
    )(*args)


def condition_kernel(place, cond, *refs):
    blocks = refs[:8]
    scale, shift, out, slots, gates, sems = refs[8:]
    width = cond.shape[1]
    share = gates.shape[1]
    copies = [
        pltpu.make_async_copy(blocks[n].at[pl.ds(4 * share, share)], slots.at[n], sems.at[n])
        for n in range(8)
    ]
    for copy in copies:
        copy.start()
    c = normalize(cond[...].astype(f32)).astype(bf16)
    out[1] = sigmoid(dot(c, scale[...]))
    out[2] = dot(c, shift[...])
    for n in range(8):
        copies[n].wait()
        gates[place[1 + n]] = slots[n]
    gate = gates[...].reshape(8 * share, 2 * width)
    out[0] = sigmoid(dot_t(c, gate[:, :width]))
    out[3] = sigmoid(dot_t(c, gate[:, width:]))


def in_vmem(count):
    return [pl.BlockSpec(memory_space=pltpu.VMEM)] * count


def condition(place, cond, weights, scale, shift):
    model = scale.shape[1]
    return pl.pallas_call(
        condition_kernel,
        in_specs=[pl.BlockSpec(memory_space=pltpu.SMEM)]
        + in_vmem(1)
        + [pl.BlockSpec(memory_space=pltpu.HBM)] * len(weights)
        + in_vmem(2),
        out_specs=pl.BlockSpec(memory_space=pltpu.VMEM),
        out_shape=jax.ShapeDtypeStruct((4, cond.shape[0], model), f32),
        scratch_shapes=[
            pltpu.VMEM((8, model // 8, model), bf16),
            pltpu.VMEM((8, model // 8, model), bf16),
            pltpu.SemaphoreType.DMA((8,)),
        ],
        compiler_params=params(58 * 1024 * 1024),
        cost_estimate=cost(4),
        name="condition",
    )(place, cond, *weights, scale, shift)


def transition_kernel(heads, acts, mix, w_out, *refs):
    out, ups, downs, sems = refs[16:]
    units = downs.shape[1]
    copies = []
    for n in range(8):
        up = refs[n].at[pl.ds(0, 2 * units)]
        copies.append(
            (
                pltpu.make_async_copy(up, ups.at[n], sems.at[0, n]),
                pltpu.make_async_copy(refs[8 + n], downs.at[n], sems.at[1, n]),
            )
        )
    for up_copy, down_copy in copies:
        up_copy.start()
        down_copy.start()
    rows = acts.shape[0]
    x = heads[...].reshape(w_out.shape[0], rows)
    attended = lax.dot_general(
        x, w_out[...], (((0,), (0,)), ((), ())), preferred_element_type=f32
    )
    stream = acts[...].astype(f32) + mix[0] * attended
    x = (mix[1] * normalize(stream) + mix[2]).astype(bf16)
    acc = jnp.zeros(stream.shape, f32)
    for n in range(8):
        copies[n][0].wait()
        both = dot_t(x, ups[n])
        up, gate = both[:, :units], both[:, units:]
        hidden = (gate * sigmoid(gate) * up).astype(bf16)
        copies[n][1].wait()
        acc = acc + dot(hidden, downs[n])
    result = (stream + mix[3] * acc).astype(bf16)
    share = out.shape[2]
    for n in range(out.shape[0]):
        out[n] = result[:, n * share : (n + 1) * share]


def transition(heads, acts, mix, w_out, ups, downs):
    rows, width = acts.shape
    units = downs[0].shape[0]
    return pl.pallas_call(
        transition_kernel,
        in_specs=in_vmem(4) + [pl.BlockSpec(memory_space=pltpu.HBM)] * 16,
        out_specs=pl.BlockSpec(memory_space=pltpu.VMEM),
        out_shape=jax.ShapeDtypeStruct((8, rows, width // 8), bf16),
        scratch_shapes=[
            pltpu.VMEM((8, 2 * units, width), bf16),
            pltpu.VMEM((8, units, width), bf16),
            pltpu.SemaphoreType.DMA((2, 8)),
        ],
        compiler_params=params(58 * 1024 * 1024),
        cost_estimate=cost(8),
        name="transition",
    )(heads, acts, mix, w_out, *ups, *downs)


def per_device(
    acts,
    cond,
    pair,
    chain_id,
    residue_mask,
    w_bias,
    chain_bias,
    ada1_scale,
    ada1_shift,
    w_qkvg,
    w_out,
    out_gate1,
    ada2_scale,
    ada2_shift,
    w_up,
    w_down,
    out_gate2,
):
    z, core, xh, y, samp = (lax.axis_index(n) for n in ("z", "core", "xh", "y", "samp"))
    samples, rows, width = acts.shape
    swap = [(0, 1), (1, 0)]
    lower = core == 0
    turn = jnp.where(lower, 1, 3)

    def around(array):
        up = [(2 * n, 2 * ((n + 1) % 8)) for n in range(8)]
        down = [(2 * n + 1, 2 * ((n + 7) % 8) + 1) for n in range(8)]
        return lax.ppermute(array, ("z", "core"), up + down)

    def around_y(array):
        up = [(n, (n + 1) % 4) for n in range(4)]
        down = [(4 + n, 4 + (n + 3) % 4) for n in range(4)]
        return lax.ppermute(array, ("core", "y"), up + down)

    def far_side(array):
        return lax.ppermute(array, ("xh", "samp"), [(0, 3), (3, 0), (1, 2), (2, 1)])

    def cross(array):
        return lax.ppermute(array, "core", swap)

    w_down_y = around_y(w_down)
    down_far = far_side(w_down)

    back, ahead = (y + 4 - turn) % 4, (y + turn) % 4
    owners = [4 * x + n for n in (y, back, ahead) for x in (xh, 1 - xh)]
    opposite = (y + 2) % 4
    owners += [4 * jnp.where(lower, xh, 1 - xh) + opposite]
    owners += [4 * jnp.where(lower, 1 - xh, xh) + opposite]
    here = jnp.stack([core] + owners).astype(jnp.int32)

    stay, send = project(here, acts, cond, ada1_scale, ada1_shift, w_qkvg.swapaxes(1, 2))
    send, w_down_y, down_far = lax.optimization_barrier((send, w_down_y, down_far))
    got = cross(send)

    def in_order(own, theirs):
        return jnp.concatenate(
            [jnp.where(lower, own, theirs), jnp.where(lower, theirs, own)], axis=0
        )

    chunk = jnp.stack([in_order(send[0], got[1]), in_order(send[1], got[0])])
    one = around(chunk)
    w_bias, w_up, chunk = lax.optimization_barrier((w_bias, w_up, chunk))
    up = jnp.concatenate(
        [
            w_up.swapaxes(1, 2).reshape(-1, width),
            jnp.concatenate([out_gate1.T, out_gate2.T], axis=1),
        ],
        axis=0,
    )
    part = up.shape[0] // 2
    up_part = far_side(lax.dynamic_slice_in_dim(up, core * part, part, 0))
    up_y = around_y(up)
    down_far_y = around_y(down_far)
    tile = tile_bias(pair, w_bias)
    tile_other = lax.ppermute(tile, "samp", swap)
    one, up_part, up_y, down_far_y, tile_other = lax.optimization_barrier(
        (one, up_part, up_y, down_far_y, tile_other)
    )
    up_far = in_order(up_part, cross(up_part))
    tiles = jnp.stack([tile, tile_other], axis=1)
    tiles = lax.all_to_all(tiles, PLANE, split_axis=0, concat_axis=0, tiled=True)
    tiles = tiles.reshape((8, 2) + tiles.shape[1:])
    two = around(one)
    one_x = cross(one)
    qg = in_order(stay, got[2])
    two, up_far, tiles = lax.optimization_barrier((two, up_far, tiles))
    side = jnp.where(lower, 1, 7)
    order = [z] + [n for s in (1, 2, 3) for n in (z + 8 * 3 - s * side, z + s * side)] + [z + 4]
    place = jnp.stack([n % 8 for n in order] + [z, core, samp]).astype(jnp.int32)
    bias = assemble(place, tiles, chain_id, residue_mask, chain_bias)
    three = around(two)
    two_x = cross(two)
    up_far_y = around_y(up_far)
    down_last = around_y(jnp.where(lower, w_down_y, down_far_y))
    parts = [(chunk, 0), (one, 0), (one_x, 1), (two, 0), (two_x, 1)]
    state = attend(qg, parts, bias, 0, None, False)
    three, state, up_far_y, down_last = lax.optimization_barrier(
        (three, state, up_far_y, down_last)
    )
    four = around(three[0])
    up_last = around_y(jnp.where(lower, up_y, up_far_y))
    three_x = cross(three)
    state = attend(qg, [(three, 0), (three_x, 1)], bias, 5, state, False)
    heads = attend(qg, [(four, None)], bias, 7, state, True)
    heads, up_last = lax.optimization_barrier((heads, up_last))

    def all_blocks(own, far, own_y, far_y, last):
        return [own, far, own_y, far_y, cross(own_y), cross(far_y), last, cross(last)]

    ups = all_blocks(up, up_far, up_y, up_far_y, up_last)
    heads = lax.all_to_all(heads, PLANE, split_axis=0, concat_axis=0, tiled=True)

    def rows_of(array):
        take, size = samples // 4, rows // 2
        at = (y * take, xh * size, 0)
        return lax.dynamic_slice(array, at, (take, size, array.shape[2])).reshape(
            take * size, array.shape[2]
        )

    mix = condition(here, rows_of(cond), ups, ada2_scale, ada2_shift)
    downs = all_blocks(w_down, down_far, w_down_y, down_far_y, down_last)
    out = transition(heads, rows_of(acts), mix, w_out, ups, downs)
    out = lax.all_to_all(out, COL, split_axis=0, concat_axis=0, tiled=True)
    out = out.reshape(2, 4, samples // 4, rows // 2, width // 8)
    return out.transpose(1, 2, 0, 3, 4).reshape(samples, rows, width // 8)


def solution(mesh):
    fine = Mesh(mesh.devices.reshape(8, 2, 2, 4, 2), ("z", "core", "xh", "y", "samp"))
    row = ("z", "core")
    in_specs = (
        P("samp", row, None),
        P("samp", row, None),
        P(row + ("samp",), COL, None),
        P(),
        P(),
        P(),
        P(COL),
        P(),
        P(),
        P(None, None, COL),
        P(),
        P(None, COL),
        P(),
        P(),
        P(None, None, COL),
        P(COL, None),
        P(None, COL),
    )
    return jax.shard_map(
        per_device,
        mesh=fine,
        in_specs=in_specs,
        out_specs=P("samp", row, COL),
        check_vma=False,
    )
```

```python
import functools
import math

import jax
import jax.numpy as jnp
from jax import lax
from jax.experimental import pallas as pl
from jax.experimental.pallas import tpu as pltpu
from jax.sharding import Mesh, PartitionSpec as P

DH = 48
PIECE = 2 * DH
GROUP = 4
WIDE = GROUP * PIECE
EPS = 1e-05
LOG2E = math.log2(math.e)
MASKED = -1000000000.0
COL = ("xh", "y")
PLANE = ("xh", "y", "core")
VMEM = 14 * 1024 * 1024

WINDOW = 256

f32 = jnp.float32
bf16 = jnp.bfloat16


def normalize(values):
    mean = jnp.mean(values, axis=-1, keepdims=True)
    square = jnp.mean(values * values, axis=-1, keepdims=True)
    return (values - mean) * lax.rsqrt(square - mean * mean + EPS)


def sigmoid(values):
    return 0.5 * jnp.tanh(0.5 * values) + 0.5


def dot(left, right):
    return jnp.dot(left, right, preferred_element_type=f32)


def dot_t(left, right):
    return lax.dot_general(left, right, (((1,), (1,)), ((), ())), preferred_element_type=f32)


def params(limit=VMEM):
    return pltpu.CompilerParams(vmem_limit_bytes=limit)


def cost(micros):
    return pl.CostEstimate(flops=0, bytes_accessed=int(micros * 3_400_000), transcendentals=0)


def project_kernel(place, acts, cond, scale, shift, w, stay, send, wcat):
    first = place[0] == 0

    @pl.when(pl.program_id(0) == 0)
    def _():
        low = [w[n, :DH] for n in range(4)]
        high = [w[n, DH:] for n in range(4)]
        kept = [jnp.where(first, low[n], high[n]) for n in (1, 2, 0, 3)]
        sent = [jnp.where(first, high[n], low[n]) for n in (1, 2, 0, 3)]
        wcat[...] = jnp.concatenate(kept + sent, axis=0)

    rows = GROUP * acts.shape[1]
    x = acts[...].reshape(rows, acts.shape[2]).astype(f32)
    c = normalize(cond[...].reshape(rows, cond.shape[2]).astype(f32)).astype(bf16)
    a = (sigmoid(dot(c, scale[...])) * normalize(x) + dot(c, shift[...])).astype(bf16)
    y = dot_t(a, wcat[...])
    lane = lax.broadcasted_iota(jnp.int32, (1, WIDE), 1) % (2 * PIECE)
    is_query = (lane >= PIECE) & (lane < PIECE + DH)
    y = (y * jnp.where(is_query, LOG2E / math.sqrt(DH), 1.0)).astype(bf16)
    step = acts.shape[1]
    for n, out in enumerate((send.at[0], stay, send.at[1], send.at[2])):
        at = n * PIECE
        out[...] = jnp.concatenate(
            [y[j * step : (j + 1) * step, at : at + PIECE] for j in range(GROUP)], axis=1
        )


def project(core, acts, cond, scale, shift, w):
    samples, rows, width = acts.shape
    groups = samples // GROUP
    one = jax.ShapeDtypeStruct((rows, samples * PIECE), bf16)
    three = jax.ShapeDtypeStruct((3,) + one.shape, bf16)
    whole = lambda shape: pl.BlockSpec(shape, lambda g, p: (0,) * len(shape))
    return pl.pallas_call(
        project_kernel,
        grid_spec=pltpu.PrefetchScalarGridSpec(
            num_scalar_prefetch=1,
            grid=(groups,),
            in_specs=[
                pl.BlockSpec((GROUP, rows, width), lambda g, p: (g, 0, 0)),
                pl.BlockSpec((GROUP, rows, cond.shape[2]), lambda g, p: (g, 0, 0)),
                whole(scale.shape),
                whole(shift.shape),
                whole(w.shape),
            ],
            out_specs=[
                pl.BlockSpec((rows, WIDE), lambda g, p: (0, g)),
                pl.BlockSpec((3, rows, WIDE), lambda g, p: (0, 0, g)),
            ],
            scratch_shapes=[pltpu.VMEM((WIDE, width), bf16)],
        ),
        out_shape=[one, three],
        compiler_params=params(56 * 1024 * 1024),
        cost_estimate=cost(8),
        name="project",
    )(core, acts, cond, scale, shift, w)


def bias_kernel(pair, w, out, left, right):
    step = pl.program_id(0)
    heads = w.shape[0]
    rows, keys = left.shape[0] // heads, pair.shape[1]
    spare = jnp.zeros((heads, 256 - keys), f32)
    for i in range(pair.shape[0]):
        x = normalize(pair[i].astype(f32)).astype(bf16)
        t = dot_t(w[...], x)
        at = pl.ds(step * pair.shape[0] + i, heads, stride=rows)
        left[at, :] = t[:, :128]
        right[at, :] = jnp.concatenate([t[:, 128:], spare], axis=1)

    @pl.when(step == pl.num_programs(0) - 1)
    def _():
        for h in range(heads):
            rest = right[h * rows : (h + 1) * rows]
            rest = jnp.concatenate([rest[: rows // 2, :64], rest[rows // 2 :, :64]], axis=1)
            tile = jnp.concatenate([left[h * rows : (h + 1) * rows], rest], axis=0).astype(bf16)
            out[h] = tile


def tile_bias(pair, w_bias):
    rows, keys, width = pair.shape
    heads = w_bias.shape[1]
    block = 8
    shape = (heads, rows * keys // 128, 128)
    return pl.pallas_call(
        bias_kernel,
        grid=(rows // block,),
        in_specs=[
            pl.BlockSpec((block, keys, width), lambda g: (g, 0, 0)),
            pl.BlockSpec((heads, width), lambda g: (0, 0)),
        ],
        out_specs=pl.BlockSpec(shape, lambda g: (0, 0, 0)),
        out_shape=jax.ShapeDtypeStruct(shape, bf16),
        scratch_shapes=[pltpu.VMEM((heads * rows, 128), f32)] * 2,
        compiler_params=params(),
        cost_estimate=cost(6),
        name="tile_bias",
    )(pair, w_bias.T)


def assemble_kernel(place, *refs):
    tiles, chains, masks = refs[:2], refs[2:4], refs[4:6]
    chain_q, cb, out = refs[6:]
    keys = out.shape[1]
    row = lax.broadcasted_iota(jnp.int32, (keys, keys), 0)
    col = lax.broadcasted_iota(jnp.int32, (keys, keys), 1)

    def upright(line):
        return jnp.sum(jnp.where(row == col, line.astype(f32), 0.0), axis=1, keepdims=True)

    query = place[8] * keys + col
    low = place[10] == 0
    for n in range(2):
        tile = tiles[n]
        parts = []
        for core in range(2):
            own, theirs = tile[0, core, 0].astype(f32), tile[0, core, 1].astype(f32)
            parts += [jnp.where(low, own, theirs), jnp.where(low, theirs, own)]
        rows = keys // 4
        first = jnp.concatenate([part[:rows] for part in parts], axis=0)
        rest = []
        for part in parts:
            rest += [part[rows:, :64], part[rows:, 64:]]
        bias = jnp.concatenate([first, jnp.concatenate(rest, axis=0)], axis=1).T
        same = upright(chains[n][0]) == chain_q[0].astype(f32)
        bias = bias + jnp.where(same, cb[place[9]], 0.0)
        key = place[2 * pl.program_id(0) + n] * keys + row
        active = (upright(masks[n][0]) == 1.0) | (query == key)
        bias = jnp.where(active, bias * LOG2E, MASKED)
        out[n] = jnp.concatenate([bias, bias], axis=1)


def assemble(place, tiles, chain_id, residue_mask, chain_bias):
    chunks, cores, halves, rows, lanes = tiles.shape
    keys = chain_id.shape[0] // chunks
    tile = [
        pl.BlockSpec((1, cores, halves, rows, lanes), lambda n, p, m=m: (p[2 * n + m], 0, 0, 0, 0))
        for m in range(2)
    ]
    line = [pl.BlockSpec((1, 1, keys), lambda n, p, m=m: (p[2 * n + m], 0, 0)) for m in range(2)]
    own = pl.BlockSpec((1, 1, keys), lambda n, p: (p[8], 0, 0))
    chain = chain_id.reshape(chunks, 1, keys)
    mask = residue_mask.reshape(chunks, 1, keys)
    return pl.pallas_call(
        assemble_kernel,
        grid_spec=pltpu.PrefetchScalarGridSpec(
            num_scalar_prefetch=1,
            grid=(chunks // 2,),
            in_specs=tile + line + line + [own, pl.BlockSpec(memory_space=pltpu.SMEM)],
            out_specs=pl.BlockSpec((2, keys, 2 * keys), lambda n, p: (n, 0, 0)),
        ),
        out_shape=jax.ShapeDtypeStruct((chunks, keys, 2 * keys), f32),
        compiler_params=params(),
        cost_estimate=cost(5),
        name="assemble",
    )(place, tiles, tiles, chain, chain, mask, mask, chain, chain_bias)


def attend_kernel(start, last, picks, begin, chunks, *refs):
    qg_ref, refs = refs[0], refs[1:]
    key_refs, refs = refs[: len(picks)], refs[len(picks) :]
    key_refs = [ref if n is None else ref.at[n] for ref, n in zip(key_refs, picks)]
    bias_ref, refs = refs[0], refs[1:]
    if not start:
        state, refs = refs[0], refs[1:]
    out = refs[0]
    rows = qg_ref.shape[0]
    bias = bias_ref[begin : begin + chunks].reshape(chunks * bias_ref.shape[1], 2 * rows)
    lane = lax.broadcasted_iota(jnp.int32, (1, WINDOW), 1)
    wide = lax.broadcasted_iota(jnp.int32, (1, 2 * rows), 1)
    row = lax.broadcasted_iota(jnp.int32, (2 * DH, 1), 0)
    none = jnp.zeros((), bf16)
    size = rows // 4
    pieces = {}
    for pair in range(2 * qg_ref.shape[1] // WIDE):
        a = pair // 2 * WIDE + 128 * (pair % 2)
        base = 2 * PIECE * pair - a
        group, at = pair // 2, pair % 2
        keys = jnp.concatenate([ref[:, a : a + WINDOW] for ref in key_refs], axis=0)
        queries = qg_ref[:, a : a + WINDOW]

        def both(offset):
            ends = [base + offset, base + offset + PIECE]
            return jnp.concatenate(
                [jnp.where((lane >= n) & (lane < n + DH), queries, none) for n in ends], axis=0
            )

        s = dot_t(keys, both(0)) + bias
        top = jnp.max(s, axis=0, keepdims=True)
        if not start:
            top_old = state[group, at, DH : DH + 1]
            top = jnp.maximum(top, top_old)
            alpha = jnp.exp2(top_old - top)
        p = jnp.exp2(s - top)
        total = jnp.sum(p, axis=0, keepdims=True)
        source = base + DH + jnp.where(row < DH, row, row + PIECE - DH)
        select = jnp.where(lane == source, 1.0, 0.0).astype(bf16)
        values = dot_t(select, keys).astype(bf16)
        o = dot(values, p.astype(bf16))
        o = jnp.where(wide < rows, o[:DH], o[DH:])
        if not start:
            total = total + alpha * state[group, at, DH + 1 : DH + 2]
            o = o + alpha * state[group, at, :DH]
        if last:
            fold = (lane == base + DH + row[:DH]) | (lane == base + DH + PIECE + row[:DH])
            gate = dot_t(jnp.where(fold, 1.0, 0.0).astype(bf16), both(DH))
            o = (o / total * sigmoid(gate)).astype(bf16)
            for j in range(2):
                for quarter in range(4):
                    first = j * rows + quarter * size
                    pieces[2 * pair + j, quarter] = o[:, first : first + size]
        else:
            out[group, at, :DH] = o
            out[group, at, DH:] = jnp.concatenate(
                [top, total, jnp.zeros((6, 2 * rows), f32)], axis=0
            )
    if last:
        for part in range(4):
            for quarter in range(4):
                core, half = quarter // 2, quarter % 2
                out[half * 8 + part * 2 + core] = jnp.concatenate(
                    [pieces[3 * part + n, quarter] for n in range(3)], axis=1
                )


def attend(qg, parts, bias, begin, state, last):
    rows, width = qg.shape
    parts, picks = zip(*parts)
    chunks = len(parts)
    args = [qg, *parts, bias] + ([] if state is None else [state])
    if last:
        out_shape = jax.ShapeDtypeStruct((16, DH, 3 * rows // 4), bf16)
    else:
        out_shape = jax.ShapeDtypeStruct((width // WIDE, 2, DH + 8, 2 * rows), f32)
    return pl.pallas_call(
        functools.partial(attend_kernel, state is None, last, picks, begin, chunks),
        in_specs=[pl.BlockSpec(memory_space=pltpu.VMEM)] * len(args),
        out_specs=pl.BlockSpec(memory_space=pltpu.VMEM),
        out_shape=out_shape,
        compiler_params=params(),
        cost_estimate=cost(2 + chunks),
        name="attend_last" if last else "attend",
    )(*args)


def condition_kernel(place, cond, *refs):
    blocks = refs[:8]
    scale, shift, out, slots, gates, sems = refs[8:]
    width = cond.shape[1]
    share = gates.shape[1]
    copies = [
        pltpu.make_async_copy(blocks[n].at[pl.ds(4 * share, share)], slots.at[n], sems.at[n])
        for n in range(8)
    ]
    for copy in copies:
        copy.start()
    c = normalize(cond[...].astype(f32)).astype(bf16)
    out[1] = sigmoid(dot(c, scale[...]))
    out[2] = dot(c, shift[...])
    for n in range(8):
        copies[n].wait()
        gates[place[1 + n]] = slots[n]
    gate = gates[...].reshape(8 * share, 2 * width)
    out[0] = sigmoid(dot_t(c, gate[:, :width]))
    out[3] = sigmoid(dot_t(c, gate[:, width:]))


def in_vmem(count):
    return [pl.BlockSpec(memory_space=pltpu.VMEM)] * count


def condition(place, cond, weights, scale, shift):
    model = scale.shape[1]
    return pl.pallas_call(
        condition_kernel,
        in_specs=[pl.BlockSpec(memory_space=pltpu.SMEM)]
        + in_vmem(1)
        + [pl.BlockSpec(memory_space=pltpu.HBM)] * len(weights)
        + in_vmem(2),
        out_specs=pl.BlockSpec(memory_space=pltpu.VMEM),
        out_shape=jax.ShapeDtypeStruct((4, cond.shape[0], model), f32),
        scratch_shapes=[
            pltpu.VMEM((8, model // 8, model), bf16),
            pltpu.VMEM((8, model // 8, model), bf16),
            pltpu.SemaphoreType.DMA((8,)),
        ],
        compiler_params=params(58 * 1024 * 1024),
        cost_estimate=cost(4),
        name="condition",
    )(place, cond, *weights, scale, shift)


def transition_kernel(heads, acts, mix, w_out, *refs):
    out, ups, downs, sems = refs[16:]
    units = downs.shape[1]
    copies = []
    for n in range(8):
        up = refs[n].at[pl.ds(0, 2 * units)]
        copies.append(
            (
                pltpu.make_async_copy(up, ups.at[n], sems.at[0, n]),
                pltpu.make_async_copy(refs[8 + n], downs.at[n], sems.at[1, n]),
            )
        )
    for up_copy, down_copy in copies:
        up_copy.start()
        down_copy.start()
    rows = acts.shape[0]
    x = heads[...].reshape(w_out.shape[0], rows)
    attended = lax.dot_general(
        x, w_out[...], (((0,), (0,)), ((), ())), preferred_element_type=f32
    )
    stream = acts[...].astype(f32) + mix[0] * attended
    x = (mix[1] * normalize(stream) + mix[2]).astype(bf16)
    acc = jnp.zeros(stream.shape, f32)
    for n in range(8):
        copies[n][0].wait()
        both = dot_t(x, ups[n])
        up, gate = both[:, :units], both[:, units:]
        hidden = (gate * sigmoid(gate) * up).astype(bf16)
        copies[n][1].wait()
        acc = acc + dot(hidden, downs[n])
    result = (stream + mix[3] * acc).astype(bf16)
    share = out.shape[2]
    for n in range(out.shape[0]):
        out[n] = result[:, n * share : (n + 1) * share]


def transition(heads, acts, mix, w_out, ups, downs):
    rows, width = acts.shape
    units = downs[0].shape[0]
    return pl.pallas_call(
        transition_kernel,
        in_specs=in_vmem(4) + [pl.BlockSpec(memory_space=pltpu.HBM)] * 16,
        out_specs=pl.BlockSpec(memory_space=pltpu.VMEM),
        out_shape=jax.ShapeDtypeStruct((8, rows, width // 8), bf16),
        scratch_shapes=[
            pltpu.VMEM((8, 2 * units, width), bf16),
            pltpu.VMEM((8, units, width), bf16),
            pltpu.SemaphoreType.DMA((2, 8)),
        ],
        compiler_params=params(58 * 1024 * 1024),
        cost_estimate=cost(8),
        name="transition",
    )(heads, acts, mix, w_out, *ups, *downs)


def per_device(
    acts,
    cond,
    pair,
    chain_id,
    residue_mask,
    w_bias,
    chain_bias,
    ada1_scale,
    ada1_shift,
    w_qkvg,
    w_out,
    out_gate1,
    ada2_scale,
    ada2_shift,
    w_up,
    w_down,
    out_gate2,
):
    z, core, xh, y, samp = (lax.axis_index(n) for n in ("z", "core", "xh", "y", "samp"))
    samples, rows, width = acts.shape
    swap = [(0, 1), (1, 0)]
    lower = core == 0
    turn = jnp.where(lower, 1, 3)

    def around(array):
        up = [(2 * n, 2 * ((n + 1) % 8)) for n in range(8)]
        down = [(2 * n + 1, 2 * ((n + 7) % 8) + 1) for n in range(8)]
        return lax.ppermute(array, ("z", "core"), up + down)

    def around_y(array):
        up = [(n, (n + 1) % 4) for n in range(4)]
        down = [(4 + n, 4 + (n + 3) % 4) for n in range(4)]
        return lax.ppermute(array, ("core", "y"), up + down)

    def far_side(array):
        return lax.ppermute(array, ("xh", "samp"), [(0, 3), (3, 0), (1, 2), (2, 1)])

    def cross(array):
        return lax.ppermute(array, "core", swap)

    w_down_y = around_y(w_down)
    down_far = far_side(w_down)

    back, ahead = (y + 4 - turn) % 4, (y + turn) % 4
    owners = [4 * x + n for n in (y, back, ahead) for x in (xh, 1 - xh)]
    opposite = (y + 2) % 4
    owners += [4 * jnp.where(lower, xh, 1 - xh) + opposite]
    owners += [4 * jnp.where(lower, 1 - xh, xh) + opposite]
    here = jnp.stack([core] + owners).astype(jnp.int32)

    stay, send = project(here, acts, cond, ada1_scale, ada1_shift, w_qkvg.swapaxes(1, 2))
    send, w_down_y, down_far = lax.optimization_barrier((send, w_down_y, down_far))
    got = cross(send)

    def in_order(own, theirs):
        return jnp.concatenate(
            [jnp.where(lower, own, theirs), jnp.where(lower, theirs, own)], axis=0
        )

    chunk = jnp.stack([in_order(send[0], got[1]), in_order(send[1], got[0])])
    one = around(chunk)
    w_bias, w_up, chunk = lax.optimization_barrier((w_bias, w_up, chunk))
    up = jnp.concatenate(
        [
            w_up.swapaxes(1, 2).reshape(-1, width),
            jnp.concatenate([out_gate1.T, out_gate2.T], axis=1),
        ],
        axis=0,
    )
    part = up.shape[0] // 2
    up_part = far_side(lax.dynamic_slice_in_dim(up, core * part, part, 0))
    up_y = around_y(up)
    down_far_y = around_y(down_far)
    tile = tile_bias(pair, w_bias)
    tile_other = lax.ppermute(tile, "samp", swap)
    one, up_part, up_y, down_far_y, tile_other = lax.optimization_barrier(
        (one, up_part, up_y, down_far_y, tile_other)
    )
    up_far = in_order(up_part, cross(up_part))
    tiles = jnp.stack([tile, tile_other], axis=1)
    tiles = lax.all_to_all(tiles, PLANE, split_axis=0, concat_axis=0, tiled=True)
    tiles = tiles.reshape((8, 2) + tiles.shape[1:])
    two = around(one)
    one_x = cross(one)
    qg = in_order(stay, got[2])
    two, up_far = lax.optimization_barrier((two, up_far))
    up_far, tiles = lax.optimization_barrier((up_far, tiles))
    side = jnp.where(lower, 1, 7)
    order = [z] + [n for s in (1, 2, 3) for n in (z + 8 * 3 - s * side, z + s * side)] + [z + 4]
    place = jnp.stack([n % 8 for n in order] + [z, core, samp]).astype(jnp.int32)
    bias = assemble(place, tiles, chain_id, residue_mask, chain_bias)
    three = around(two)
    two_x = cross(two)
    up_far_y = around_y(up_far)
    down_last = around_y(jnp.where(lower, w_down_y, down_far_y))
    parts = [(chunk, 0), (one, 0), (one_x, 1), (two, 0), (two_x, 1)]
    state = attend(qg, parts, bias, 0, None, False)
    state, up_far_y, down_last = lax.optimization_barrier((state, up_far_y, down_last))
    four = around(three[0])
    up_last = around_y(jnp.where(lower, up_y, up_far_y))
    three_x = cross(three)
    state = attend(qg, [(three, 0), (three_x, 1)], bias, 5, state, False)
    heads = attend(qg, [(four, None)], bias, 7, state, True)
    heads, up_last = lax.optimization_barrier((heads, up_last))

    def all_blocks(own, far, own_y, far_y, last):
        return [own, far, own_y, far_y, cross(own_y), cross(far_y), last, cross(last)]

    ups = all_blocks(up, up_far, up_y, up_far_y, up_last)
    heads = lax.all_to_all(heads, PLANE, split_axis=0, concat_axis=0, tiled=True)

    def rows_of(array):
        take, size = samples // 4, rows // 2
        at = (y * take, xh * size, 0)
        return lax.dynamic_slice(array, at, (take, size, array.shape[2])).reshape(
            take * size, array.shape[2]
        )

    mix = condition(here, rows_of(cond), ups, ada2_scale, ada2_shift)
    downs = all_blocks(w_down, down_far, w_down_y, down_far_y, down_last)
    out = transition(heads, rows_of(acts), mix, w_out, ups, downs)
    out = lax.all_to_all(out, COL, split_axis=0, concat_axis=0, tiled=True)
    out = out.reshape(2, 4, samples // 4, rows // 2, width // 8)
    return out.transpose(1, 2, 0, 3, 4).reshape(samples, rows, width // 8)


def solution(mesh):
    fine = Mesh(mesh.devices.reshape(8, 2, 2, 4, 2), ("z", "core", "xh", "y", "samp"))
    row = ("z", "core")
    in_specs = (
        P("samp", row, None),
        P("samp", row, None),
        P(row + ("samp",), COL, None),
        P(),
        P(),
        P(),
        P(COL),
        P(),
        P(),
        P(None, None, COL),
        P(),
        P(None, COL),
        P(),
        P(),
        P(None, None, COL),
        P(COL, None),
        P(None, COL),
    )
    return jax.shard_map(
        per_device,
        mesh=fine,
        in_specs=in_specs,
        out_specs=P("samp", row, COL),
        check_vma=False,
    )
```

```python
import functools
import math

import jax
import jax.numpy as jnp
from jax import lax
from jax.experimental import pallas as pl
from jax.experimental.pallas import tpu as pltpu
from jax.sharding import Mesh, PartitionSpec as P

DH = 48
PIECE = 2 * DH
GROUP = 4
WIDE = GROUP * PIECE
EPS = 1e-05
LOG2E = math.log2(math.e)
MASKED = -1000000000.0
COL = ("xh", "y")
PLANE = ("xh", "y", "core")
VMEM = 14 * 1024 * 1024

WINDOW = 256

f32 = jnp.float32
bf16 = jnp.bfloat16


def normalize(values):
    mean = jnp.mean(values, axis=-1, keepdims=True)
    square = jnp.mean(values * values, axis=-1, keepdims=True)
    return (values - mean) * lax.rsqrt(square - mean * mean + EPS)


def sigmoid(values):
    return 0.5 * jnp.tanh(0.5 * values) + 0.5


def dot(left, right):
    return jnp.dot(left, right, preferred_element_type=f32)


def dot_t(left, right):
    return lax.dot_general(left, right, (((1,), (1,)), ((), ())), preferred_element_type=f32)


def params(limit=VMEM):
    return pltpu.CompilerParams(vmem_limit_bytes=limit)


def cost(micros):
    return pl.CostEstimate(flops=0, bytes_accessed=int(micros * 3_400_000), transcendentals=0)


def project_kernel(place, acts, cond, scale, shift, w, stay, send, wcat):
    first = place[0] == 0

    @pl.when(pl.program_id(0) == 0)
    def _():
        low = [w[n, :DH] for n in range(4)]
        high = [w[n, DH:] for n in range(4)]
        kept = [jnp.where(first, low[n], high[n]) for n in (1, 2, 0, 3)]
        sent = [jnp.where(first, high[n], low[n]) for n in (1, 2, 0, 3)]
        wcat[...] = jnp.concatenate(kept + sent, axis=0)

    rows = GROUP * acts.shape[1]
    x = acts[...].reshape(rows, acts.shape[2]).astype(f32)
    c = normalize(cond[...].reshape(rows, cond.shape[2]).astype(f32)).astype(bf16)
    a = (sigmoid(dot(c, scale[...])) * normalize(x) + dot(c, shift[...])).astype(bf16)
    y = dot_t(a, wcat[...])
    lane = lax.broadcasted_iota(jnp.int32, (1, WIDE), 1) % (2 * PIECE)
    is_query = (lane >= PIECE) & (lane < PIECE + DH)
    y = (y * jnp.where(is_query, LOG2E / math.sqrt(DH), 1.0)).astype(bf16)
    step = acts.shape[1]
    for n, out in enumerate((send.at[0], stay, send.at[1], send.at[2])):
        at = n * PIECE
        out[...] = jnp.concatenate(
            [y[j * step : (j + 1) * step, at : at + PIECE] for j in range(GROUP)], axis=1
        )


def project(core, acts, cond, scale, shift, w):
    samples, rows, width = acts.shape
    groups = samples // GROUP
    one = jax.ShapeDtypeStruct((rows, samples * PIECE), bf16)
    three = jax.ShapeDtypeStruct((3,) + one.shape, bf16)
    whole = lambda shape: pl.BlockSpec(shape, lambda g, p: (0,) * len(shape))
    return pl.pallas_call(
        project_kernel,
        grid_spec=pltpu.PrefetchScalarGridSpec(
            num_scalar_prefetch=1,
            grid=(groups,),
            in_specs=[
                pl.BlockSpec((GROUP, rows, width), lambda g, p: (g, 0, 0)),
                pl.BlockSpec((GROUP, rows, cond.shape[2]), lambda g, p: (g, 0, 0)),
                whole(scale.shape),
                whole(shift.shape),
                whole(w.shape),
            ],
            out_specs=[
                pl.BlockSpec((rows, WIDE), lambda g, p: (0, g)),
                pl.BlockSpec((3, rows, WIDE), lambda g, p: (0, 0, g)),
            ],
            scratch_shapes=[pltpu.VMEM((WIDE, width), bf16)],
        ),
        out_shape=[one, three],
        compiler_params=params(56 * 1024 * 1024),
        cost_estimate=cost(8),
        name="project",
    )(core, acts, cond, scale, shift, w)


def bias_kernel(pair, w, out, left, right):
    step = pl.program_id(0)
    heads = w.shape[0]
    rows, keys = left.shape[0] // heads, pair.shape[1]
    spare = jnp.zeros((heads, 256 - keys), f32)
    for i in range(pair.shape[0]):
        x = normalize(pair[i].astype(f32)).astype(bf16)
        t = dot_t(w[...], x)
        at = pl.ds(step * pair.shape[0] + i, heads, stride=rows)
        left[at, :] = t[:, :128]
        right[at, :] = jnp.concatenate([t[:, 128:], spare], axis=1)

    @pl.when(step == pl.num_programs(0) - 1)
    def _():
        for h in range(heads):
            rest = right[h * rows : (h + 1) * rows]
            rest = jnp.concatenate([rest[: rows // 2, :64], rest[rows // 2 :, :64]], axis=1)
            tile = jnp.concatenate([left[h * rows : (h + 1) * rows], rest], axis=0).astype(bf16)
            out[h] = tile


def tile_bias(pair, w_bias):
    rows, keys, width = pair.shape
    heads = w_bias.shape[1]
    block = 8
    shape = (heads, rows * keys // 128, 128)
    return pl.pallas_call(
        bias_kernel,
        grid=(rows // block,),
        in_specs=[
            pl.BlockSpec((block, keys, width), lambda g: (g, 0, 0)),
            pl.BlockSpec((heads, width), lambda g: (0, 0)),
        ],
        out_specs=pl.BlockSpec(shape, lambda g: (0, 0, 0)),
        out_shape=jax.ShapeDtypeStruct(shape, bf16),
        scratch_shapes=[pltpu.VMEM((heads * rows, 128), f32)] * 2,
        compiler_params=params(),
        cost_estimate=cost(6),
        name="tile_bias",
    )(pair, w_bias.T)


def assemble_kernel(place, *refs):
    tiles, chains, masks = refs[:2], refs[2:4], refs[4:6]
    chain_q, cb, out = refs[6:]
    keys = out.shape[1]
    row = lax.broadcasted_iota(jnp.int32, (keys, keys), 0)
    col = lax.broadcasted_iota(jnp.int32, (keys, keys), 1)

    def upright(line):
        return jnp.sum(jnp.where(row == col, line.astype(f32), 0.0), axis=1, keepdims=True)

    query = place[8] * keys + col
    low = place[10] == 0
    for n in range(2):
        tile = tiles[n]
        parts = []
        for core in range(2):
            own, theirs = tile[0, core, 0].astype(f32), tile[0, core, 1].astype(f32)
            parts += [jnp.where(low, own, theirs), jnp.where(low, theirs, own)]
        rows = keys // 4
        first = jnp.concatenate([part[:rows] for part in parts], axis=0)
        rest = []
        for part in parts:
            rest += [part[rows:, :64], part[rows:, 64:]]
        bias = jnp.concatenate([first, jnp.concatenate(rest, axis=0)], axis=1).T
        same = upright(chains[n][0]) == chain_q[0].astype(f32)
        bias = bias + jnp.where(same, cb[place[9]], 0.0)
        key = place[2 * pl.program_id(0) + n] * keys + row
        active = (upright(masks[n][0]) == 1.0) | (query == key)
        bias = jnp.where(active, bias * LOG2E, MASKED)
        out[n] = jnp.concatenate([bias, bias], axis=1)


def assemble(place, tiles, chain_id, residue_mask, chain_bias):
    chunks, cores, halves, rows, lanes = tiles.shape
    keys = chain_id.shape[0] // chunks
    tile = [
        pl.BlockSpec((1, cores, halves, rows, lanes), lambda n, p, m=m: (p[2 * n + m], 0, 0, 0, 0))
        for m in range(2)
    ]
    line = [pl.BlockSpec((1, 1, keys), lambda n, p, m=m: (p[2 * n + m], 0, 0)) for m in range(2)]
    own = pl.BlockSpec((1, 1, keys), lambda n, p: (p[8], 0, 0))
    chain = chain_id.reshape(chunks, 1, keys)
    mask = residue_mask.reshape(chunks, 1, keys)
    return pl.pallas_call(
        assemble_kernel,
        grid_spec=pltpu.PrefetchScalarGridSpec(
            num_scalar_prefetch=1,
            grid=(chunks // 2,),
            in_specs=tile + line + line + [own, pl.BlockSpec(memory_space=pltpu.SMEM)],
            out_specs=pl.BlockSpec((2, keys, 2 * keys), lambda n, p: (n, 0, 0)),
        ),
        out_shape=jax.ShapeDtypeStruct((chunks, keys, 2 * keys), f32),
        compiler_params=params(),
        cost_estimate=cost(5),
        name="assemble",
    )(place, tiles, tiles, chain, chain, mask, mask, chain, chain_bias)


def attend_kernel(start, last, picks, begin, chunks, *refs):
    qg_ref, refs = refs[0], refs[1:]
    key_refs, refs = refs[: len(picks)], refs[len(picks) :]
    key_refs = [ref if n is None else ref.at[n] for ref, n in zip(key_refs, picks)]
    bias_ref, refs = refs[0], refs[1:]
    if not start:
        state, refs = refs[0], refs[1:]
    out = refs[0]
    rows = qg_ref.shape[0]
    bias = bias_ref[begin : begin + chunks].reshape(chunks * bias_ref.shape[1], 2 * rows)
    lane = lax.broadcasted_iota(jnp.int32, (1, WINDOW), 1)
    wide = lax.broadcasted_iota(jnp.int32, (1, 2 * rows), 1)
    row = lax.broadcasted_iota(jnp.int32, (2 * DH, 1), 0)
    none = jnp.zeros((), bf16)
    size = rows // 4
    pieces = {}
    for pair in range(2 * qg_ref.shape[1] // WIDE):
        a = pair // 2 * WIDE + 128 * (pair % 2)
        base = 2 * PIECE * pair - a
        group, at = pair // 2, pair % 2
        keys = jnp.concatenate([ref[:, a : a + WINDOW] for ref in key_refs], axis=0)
        queries = qg_ref[:, a : a + WINDOW]

        def both(offset):
            ends = [base + offset, base + offset + PIECE]
            return jnp.concatenate(
                [jnp.where((lane >= n) & (lane < n + DH), queries, none) for n in ends], axis=0
            )

        s = dot_t(keys, both(0)) + bias
        top = jnp.max(s, axis=0, keepdims=True)
        if not start:
            top_old = state[group, at, DH : DH + 1]
            top = jnp.maximum(top, top_old)
            alpha = jnp.exp2(top_old - top)
        p = jnp.exp2(s - top)
        total = jnp.sum(p, axis=0, keepdims=True)
        source = base + DH + jnp.where(row < DH, row, row + PIECE - DH)
        select = jnp.where(lane == source, 1.0, 0.0).astype(bf16)
        values = dot_t(select, keys).astype(bf16)
        o = dot(values, p.astype(bf16))
        o = jnp.where(wide < rows, o[:DH], o[DH:])
        if not start:
            total = total + alpha * state[group, at, DH + 1 : DH + 2]
            o = o + alpha * state[group, at, :DH]
        if last:
            fold = (lane == base + DH + row[:DH]) | (lane == base + DH + PIECE + row[:DH])
            gate = dot_t(jnp.where(fold, 1.0, 0.0).astype(bf16), both(DH))
            o = (o / total * sigmoid(gate)).astype(bf16)
            for j in range(2):
                for quarter in range(4):
                    first = j * rows + quarter * size
                    pieces[2 * pair + j, quarter] = o[:, first : first + size]
        else:
            out[group, at, :DH] = o
            out[group, at, DH:] = jnp.concatenate(
                [top, total, jnp.zeros((6, 2 * rows), f32)], axis=0
            )
    if last:
        for part in range(4):
            for quarter in range(4):
                core, half = quarter // 2, quarter % 2
                out[half * 8 + part * 2 + core] = jnp.concatenate(
                    [pieces[3 * part + n, quarter] for n in range(3)], axis=1
                )


def attend(qg, parts, bias, begin, state, last):
    rows, width = qg.shape
    parts, picks = zip(*parts)
    chunks = len(parts)
    args = [qg, *parts, bias] + ([] if state is None else [state])
    if last:
        out_shape = jax.ShapeDtypeStruct((16, DH, 3 * rows // 4), bf16)
    else:
        out_shape = jax.ShapeDtypeStruct((width // WIDE, 2, DH + 8, 2 * rows), f32)
    return pl.pallas_call(
        functools.partial(attend_kernel, state is None, last, picks, begin, chunks),
        in_specs=[pl.BlockSpec(memory_space=pltpu.VMEM)] * len(args),
        out_specs=pl.BlockSpec(memory_space=pltpu.VMEM),
        out_shape=out_shape,
        compiler_params=params(),
        cost_estimate=cost(2 + chunks),
        name="attend_last" if last else "attend",
    )(*args)


def condition_kernel(place, cond, *refs):
    blocks = refs[:8]
    scale, shift, out, slots, gates, sems = refs[8:]
    width = cond.shape[1]
    share = gates.shape[1]
    copies = [
        pltpu.make_async_copy(blocks[n].at[pl.ds(4 * share, share)], slots.at[n], sems.at[n])
        for n in range(8)
    ]
    for copy in copies:
        copy.start()
    c = normalize(cond[...].astype(f32)).astype(bf16)
    out[1] = sigmoid(dot(c, scale[...]))
    out[2] = dot(c, shift[...])
    for n in range(8):
        copies[n].wait()
        gates[place[1 + n]] = slots[n]
    gate = gates[...].reshape(8 * share, 2 * width)
    out[0] = sigmoid(dot_t(c, gate[:, :width]))
    out[3] = sigmoid(dot_t(c, gate[:, width:]))


def in_vmem(count):
    return [pl.BlockSpec(memory_space=pltpu.VMEM)] * count


def condition(place, cond, weights, scale, shift):
    model = scale.shape[1]
    return pl.pallas_call(
        condition_kernel,
        in_specs=[pl.BlockSpec(memory_space=pltpu.SMEM)]
        + in_vmem(1)
        + [pl.BlockSpec(memory_space=pltpu.HBM)] * len(weights)
        + in_vmem(2),
        out_specs=pl.BlockSpec(memory_space=pltpu.VMEM),
        out_shape=jax.ShapeDtypeStruct((4, cond.shape[0], model), f32),
        scratch_shapes=[
            pltpu.VMEM((8, model // 8, model), bf16),
            pltpu.VMEM((8, model // 8, model), bf16),
            pltpu.SemaphoreType.DMA((8,)),
        ],
        compiler_params=params(58 * 1024 * 1024),
        cost_estimate=cost(4),
        name="condition",
    )(place, cond, *weights, scale, shift)


def transition_kernel(heads, acts, mix, w_out, *refs):
    out, ups, downs, sems = refs[16:]
    units = downs.shape[1]
    copies = []
    for n in range(8):
        up = refs[n].at[pl.ds(0, 2 * units)]
        copies.append(
            (
                pltpu.make_async_copy(up, ups.at[n], sems.at[0, n]),
                pltpu.make_async_copy(refs[8 + n], downs.at[n], sems.at[1, n]),
            )
        )
    for up_copy, down_copy in copies:
        up_copy.start()
        down_copy.start()
    rows = acts.shape[0]
    x = heads[...].reshape(w_out.shape[0], rows)
    attended = lax.dot_general(
        x, w_out[...], (((0,), (0,)), ((), ())), preferred_element_type=f32
    )
    stream = acts[...].astype(f32) + mix[0] * attended
    x = (mix[1] * normalize(stream) + mix[2]).astype(bf16)
    acc = jnp.zeros(stream.shape, f32)
    for n in range(8):
        copies[n][0].wait()
        both = dot_t(x, ups[n])
        up, gate = both[:, :units], both[:, units:]
        hidden = (gate * sigmoid(gate) * up).astype(bf16)
        copies[n][1].wait()
        acc = acc + dot(hidden, downs[n])
    result = (stream + mix[3] * acc).astype(bf16)
    share = out.shape[2]
    for n in range(out.shape[0]):
        out[n] = result[:, n * share : (n + 1) * share]


def transition(heads, acts, mix, w_out, ups, downs):
    rows, width = acts.shape
    units = downs[0].shape[0]
    return pl.pallas_call(
        transition_kernel,
        in_specs=in_vmem(4) + [pl.BlockSpec(memory_space=pltpu.HBM)] * 16,
        out_specs=pl.BlockSpec(memory_space=pltpu.VMEM),
        out_shape=jax.ShapeDtypeStruct((8, rows, width // 8), bf16),
        scratch_shapes=[
            pltpu.VMEM((8, 2 * units, width), bf16),
            pltpu.VMEM((8, units, width), bf16),
            pltpu.SemaphoreType.DMA((2, 8)),
        ],
        compiler_params=params(58 * 1024 * 1024),
        cost_estimate=cost(8),
        name="transition",
    )(heads, acts, mix, w_out, *ups, *downs)


def per_device(
    acts,
    cond,
    pair,
    chain_id,
    residue_mask,
    w_bias,
    chain_bias,
    ada1_scale,
    ada1_shift,
    w_qkvg,
    w_out,
    out_gate1,
    ada2_scale,
    ada2_shift,
    w_up,
    w_down,
    out_gate2,
):
    z, core, xh, y, samp = (lax.axis_index(n) for n in ("z", "core", "xh", "y", "samp"))
    samples, rows, width = acts.shape
    swap = [(0, 1), (1, 0)]
    lower = core == 0
    turn = jnp.where(lower, 1, 3)

    def around(array):
        up = [(2 * n, 2 * ((n + 1) % 8)) for n in range(8)]
        down = [(2 * n + 1, 2 * ((n + 7) % 8) + 1) for n in range(8)]
        return lax.ppermute(array, ("z", "core"), up + down)

    def around_y(array):
        up = [(n, (n + 1) % 4) for n in range(4)]
        down = [(4 + n, 4 + (n + 3) % 4) for n in range(4)]
        return lax.ppermute(array, ("core", "y"), up + down)

    def far_side(array):
        return lax.ppermute(array, ("xh", "samp"), [(0, 3), (3, 0), (1, 2), (2, 1)])

    def cross(array):
        return lax.ppermute(array, "core", swap)

    w_down_y = around_y(w_down)
    down_far = far_side(w_down)

    back, ahead = (y + 4 - turn) % 4, (y + turn) % 4
    owners = [4 * x + n for n in (y, back, ahead) for x in (xh, 1 - xh)]
    opposite = (y + 2) % 4
    owners += [4 * jnp.where(lower, xh, 1 - xh) + opposite]
    owners += [4 * jnp.where(lower, 1 - xh, xh) + opposite]
    here = jnp.stack([core] + owners).astype(jnp.int32)

    stay, send = project(here, acts, cond, ada1_scale, ada1_shift, w_qkvg.swapaxes(1, 2))
    send, w_down_y, down_far = lax.optimization_barrier((send, w_down_y, down_far))
    got = cross(send)

    def in_order(own, theirs):
        return jnp.concatenate(
            [jnp.where(lower, own, theirs), jnp.where(lower, theirs, own)], axis=0
        )

    chunk = jnp.stack([in_order(send[0], got[1]), in_order(send[1], got[0])])
    one = around(chunk)
    w_bias, w_up, chunk = lax.optimization_barrier((w_bias, w_up, chunk))
    up = jnp.concatenate(
        [
            w_up.swapaxes(1, 2).reshape(-1, width),
            jnp.concatenate([out_gate1.T, out_gate2.T], axis=1),
        ],
        axis=0,
    )
    part = up.shape[0] // 2
    up_part = far_side(lax.dynamic_slice_in_dim(up, core * part, part, 0))
    up_y = around_y(up)
    down_far_y = around_y(down_far)
    tile = tile_bias(pair, w_bias)
    tile_other = lax.ppermute(tile, "samp", swap)
    one, up_part, up_y, down_far_y, tile_other = lax.optimization_barrier(
        (one, up_part, up_y, down_far_y, tile_other)
    )
    up_far = in_order(up_part, cross(up_part))
    tiles = jnp.stack([tile, tile_other], axis=1)
    tiles = lax.all_to_all(tiles, PLANE, split_axis=0, concat_axis=0, tiled=True)
    tiles = tiles.reshape((8, 2) + tiles.shape[1:])
    two = around(one)
    one_x = cross(one)
    qg = in_order(stay, got[2])
    two, up_far = lax.optimization_barrier((two, up_far))
    up_far, tiles = lax.optimization_barrier((up_far, tiles))
    side = jnp.where(lower, 1, 7)
    order = [z] + [n for s in (1, 2, 3) for n in (z + 8 * 3 - s * side, z + s * side)] + [z + 4]
    place = jnp.stack([n % 8 for n in order] + [z, core, samp]).astype(jnp.int32)
    bias = assemble(place, tiles, chain_id, residue_mask, chain_bias)
    three = around(two)
    two_x = cross(two)
    up_far_y = around_y(up_far)
    down_last = around_y(jnp.where(lower, w_down_y, down_far_y))
    parts = [(chunk, 0), (one, 0), (one_x, 1), (two, 0), (two_x, 1)]
    state = attend(qg, parts, bias, 0, None, False)
    state, three = lax.optimization_barrier((state, three))
    four = around(three[0])
    up_last = around_y(jnp.where(lower, up_y, up_far_y))
    three_x = cross(three)
    state = attend(qg, [(three, 0), (three_x, 1)], bias, 5, state, False)
    heads = attend(qg, [(four, None)], bias, 7, state, True)
    heads, up_last = lax.optimization_barrier((heads, up_last))

    def all_blocks(own, far, own_y, far_y, last):
        return [own, far, own_y, far_y, cross(own_y), cross(far_y), last, cross(last)]

    ups = all_blocks(up, up_far, up_y, up_far_y, up_last)
    heads = lax.all_to_all(heads, PLANE, split_axis=0, concat_axis=0, tiled=True)

    def rows_of(array):
        take, size = samples // 4, rows // 2
        at = (y * take, xh * size, 0)
        return lax.dynamic_slice(array, at, (take, size, array.shape[2])).reshape(
            take * size, array.shape[2]
        )

    mix = condition(here, rows_of(cond), ups, ada2_scale, ada2_shift)
    downs = all_blocks(w_down, down_far, w_down_y, down_far_y, down_last)
    out = transition(heads, rows_of(acts), mix, w_out, ups, downs)
    out = lax.all_to_all(out, COL, split_axis=0, concat_axis=0, tiled=True)
    out = out.reshape(2, 4, samples // 4, rows // 2, width // 8)
    return out.transpose(1, 2, 0, 3, 4).reshape(samples, rows, width // 8)


def solution(mesh):
    fine = Mesh(mesh.devices.reshape(8, 2, 2, 4, 2), ("z", "core", "xh", "y", "samp"))
    row = ("z", "core")
    in_specs = (
        P("samp", row, None),
        P("samp", row, None),
        P(row + ("samp",), COL, None),
        P(),
        P(),
        P(),
        P(COL),
        P(),
        P(),
        P(None, None, COL),
        P(),
        P(None, COL),
        P(),
        P(),
        P(None, None, COL),
        P(COL, None),
        P(None, COL),
    )
    return jax.shard_map(
        per_device,
        mesh=fine,
        in_specs=in_specs,
        out_specs=P("samp", row, COL),
        check_vma=False,
    )
```
